32 devices in a mesh: comp: 2 (over core), lat: 4 (over z), lon: 4 (over y, x).
Axes of the slice: x: 2, y: 2, z: 4, core: 2. Of those that a mesh axis runs over, the one named last changes fastest.
Arguments:
- increment: float32 [2, 8, 64, 2048], P('comp', None, 'lat', 'lon'), may hold values from -6 to 6
- diffusivity: float32 [2, 8, 64, 2048], P('comp', None, 'lat', 'lon'), may hold values from 0.03 to 0.24
- innovation: float32 [2, 8, 64, 2048], P('comp', None, 'lat', 'lon'), may hold values from -6 to 6
- land_mask: int32 [64, 2048], P('lat', 'lon'), may hold values 0 or 1
- pull_cells: int32 [2, 4, 4, 4, 8192], P('comp', 'lat', 'lon'), may hold values from 0 to 8191
- put_cells: int32 [2, 4, 4, 4, 8192], P('comp', 'lat', 'lon'), may hold values from 0 to 8191
- pull_weight: float32 [2, 4, 4, 4, 8192], P('comp', 'lat', 'lon'), may hold values from 0.2 to 0.8
- pull_count: int32 [2, 4, 4, 4], P('comp', 'lat', 'lon'), may hold values from 1 to 8192, 16384 in all within a row
Outputs:
- linear_state: float32 [2, 8, 64, 2048], P('comp', None, 'lat', 'lon')
- gradient: float32 [2, 8, 64, 2048], P('comp', None, 'lat', 'lon')
The draws below stay inside these ranges and needn't reach their ends.
Inputs may be any that keep to these rules, and one draw needn't show every extreme that they name: `pull_count`: for each receiving block the counts over the 4 source bands add up to 16384, and the largest of them is 8192.
All inputs are finite; a program needn't handle non-finite values. No bound on the sum of `land_mask` on one device may be relied on, other than what follows from the above.
Results may differ from the reference program's by a relative error of at most 0.00002.
Values sent between devices are 32-bit elements; how exact they have to be, the bound alone decides.
A program may use at most 64 MiB of HBM per device.

```python
import math
import jax
import jax.numpy as jnp
import numpy as np

CLAT = 16
CLON = 512
LEV = 8
NSTEP = 4
NLAT = 64
NLON = 2048
CAP = 8192
N_LAT = 4
N_LON = 4


def with_ends(entries, stream_key, least, largest):
    place = [jax.random.randint(jax.random.fold_in(stream_key, axis), (), 0, length) for axis, length in enumerate(entries.shape)]
    widest = entries.shape.index(max(entries.shape))
    next_to = place[:widest] + [(place[widest] + 1) % entries.shape[widest]] + place[widest + 1:]
    return entries.at[tuple(place)].set(least).at[tuple(next_to)].set(largest)


def block_levels(stream_key, extent, shards, least, largest):
    def one(axis_at, blocks):
        steps = jax.random.uniform(jax.random.fold_in(jax.random.fold_in(stream_key, 6), axis_at), (blocks,), jnp.float32, least / len(shards), largest / len(shards))
        return jnp.repeat(jnp.exp(steps), extent[axis_at] // blocks).reshape((-1,) + (1,) * (len(extent) - axis_at - 1))

    level = one(*shards[0])
    for cut in shards[1:]:
        level = level * one(*cut)
    return level


def profile(count, total, bound, lean):
    loads = [(1 << 20) // math.isqrt(grade ** lean) + 1 for grade in range(2, count + 1)]
    rest, counts = total - bound - (count - 1), [1] * (count - 1)
    while rest > 0:
        movable = [i for i in range(count - 1) if counts[i] < bound]
        pool, left = sum([loads[i] for i in movable]), rest
        for i in movable:
            extra = min(bound - counts[i], max(1, left * loads[i] // pool), rest)
            counts[i] = counts[i] + extra
            rest = rest - extra
    return np.array([bound] + counts)


def ragged(own_key, number_of, total, most, skew):
    if number_of == 2:
        one = jax.random.randint(own_key, (), max(1, total - most), min(most, total - 1) + 1)
        return jnp.stack([one, total - one])
    sizes = jnp.asarray(profile(number_of, total, most, skew), jnp.int32)
    couples = (number_of - 1) // 2
    giver, sink = sizes[1:1 + 2 * couples:2], sizes[2:2 + 2 * couples:2]
    margin = jnp.minimum(giver - 1, most - sink)
    shifted = jax.random.randint(jax.random.fold_in(own_key, 1), (couples,), 0, 1 << 20) % (margin + 1)
    sizes = sizes.at[1:1 + 2 * couples:2].set(giver - shifted).at[2:2 + 2 * couples:2].set(sink + shifted)
    return sizes[jax.random.permutation(jax.random.fold_in(own_key, 2), number_of)]


def centred(own_key, extent, width, limit, cuts=(), kind=jnp.bfloat16):
    loudness = block_levels(own_key, extent, cuts, -0.22, 0.18) if cuts else 1.0
    result = jax.random.normal(own_key, extent, jnp.float32) * width * loudness
    return jnp.minimum(jnp.maximum(result, -limit), limit).astype(kind)


def setup_inputs(seed: int = 0) -> dict:
    seeds = jax.random.split(jax.random.key(seed), 9)
    return {
        "increment": centred(seeds[0], (2, LEV, NLAT, NLON), 1.0, 6.0, ((0, 2), (2, 4), (3, 4)), jnp.float32),
        "diffusivity": jnp.clip(jnp.exp(math.log(0.24) - 2.0794415 * jax.random.uniform(seeds[1], (2, LEV, NLAT, NLON), jnp.float32) ** block_levels(seeds[1], (2, LEV, NLAT, NLON), ((0, 2), (2, 4), (3, 4)), -0.2, 0.2)), 0.03, 0.24),
        "innovation": centred(seeds[2], (2, LEV, NLAT, NLON), 1.0, 6.0, ((0, 2), (2, 4), (3, 4)), jnp.float32),
        "land_mask": with_ends((jax.random.randint(seeds[3], (NLAT, NLON), 0, 10) < 7).astype(jnp.int32), jax.random.fold_in(seeds[3], 1), 0, 1),
        "pull_cells": with_ends(jax.random.randint(seeds[4], (2, N_LAT, N_LON, N_LAT, CAP), 0, CLAT * CLON), jax.random.fold_in(seeds[4], 1), 0, (CLAT * CLON) - 1).astype(jnp.int32),
        "put_cells": with_ends(jax.random.randint(seeds[5], (2, N_LAT, N_LON, N_LAT, CAP), 0, CLAT * CLON), jax.random.fold_in(seeds[5], 1), 0, (CLAT * CLON) - 1).astype(jnp.int32),
        "pull_weight": jnp.clip(0.2 + 0.6 * jax.random.uniform(seeds[6], (2, N_LAT, N_LON, N_LAT, CAP), jnp.float32) ** block_levels(seeds[6], (2, N_LAT, N_LON, N_LAT, CAP), ((0, 2), (1, 4), (2, 4)), -0.2, 0.2), 0.2, 0.8),
        "pull_count": jax.vmap(lambda own: ragged(own, N_LAT, 2 * CLAT * CLON, CAP, 2))(jax.random.split(seeds[7], 2 * N_LAT * N_LON)).reshape((2, N_LAT, N_LON, N_LAT)).astype(jnp.int32),
    }


def beside_all(field):
    east = jnp.roll(field, -1, axis=3)
    west = jnp.roll(field, 1, axis=3)
    south = jnp.concatenate([jnp.zeros_like(field[:, :, :1, :]), field[:, :, :-1, :]], axis=2)
    folded = jnp.stack([jnp.zeros_like(field[0, :, -1, :]), field[1, :, -1, ::-1]])[:, :, None, :]
    north = jnp.concatenate([field[:, :, 1:, :], folded], axis=2)
    return (east, west, south, north)

def advance(field, coefficients):
    east, west, south, north = beside_all(field)
    change = coefficients[0] * (east - field) + coefficients[1] * (west - field)
    change = change + coefficients[2] * (south - field)
    change = change + coefficients[3] * (north - field)
    return field + change

def couple(field, mask_plane, pull_cells, put_cells, live_weight):
    cells = CLAT * CLON
    surface = mask_plane * field[:, 0]
    blocks = surface.reshape(2, N_LAT, CLAT, N_LON, CLON).transpose(0, 1, 3, 2, 4).reshape(2, N_LAT, N_LON, cells)
    source = blocks[::-1]
    comp_index = jnp.arange(2, dtype=jnp.int32)[:, None, None, None, None]
    band_index = jnp.arange(N_LAT, dtype=jnp.int32)[None, :, None, None, None]
    column_index = jnp.arange(N_LON, dtype=jnp.int32)[None, None, :, None, None]
    source_band = jnp.arange(N_LAT, dtype=jnp.int32)[None, None, None, :, None]
    values = source[comp_index, source_band, column_index, pull_cells]
    target = ((comp_index * N_LAT + band_index) * N_LON + column_index) * cells + put_cells
    income = jax.ops.segment_sum((live_weight * values).reshape(-1), target.reshape(-1), num_segments=2 * N_LAT * N_LON * cells)
    income = income.reshape(2, N_LAT, N_LON, CLAT, CLON).transpose(0, 1, 3, 2, 4).reshape(2, NLAT, NLON)
    return field.at[:, 0].add(mask_plane * income)

def reference(increment, diffusivity, innovation, land_mask, pull_cells, put_cells, pull_weight, pull_count):
    mask_plane = jnp.stack([jnp.ones((NLAT, NLON), jnp.float32), land_mask.astype(jnp.float32)])
    mask_levels = mask_plane[:, None]
    stacked = jnp.concatenate([diffusivity, mask_levels], axis=1)
    near = beside_all(stacked)
    coefficients = [mask_levels * side[:, -1:] * 0.5 * (diffusivity + side[:, :-1]) for side in near]
    live = jnp.arange(CAP, dtype=jnp.int32) < pull_count[..., None]
    live_weight = jnp.where(live, pull_weight, jnp.zeros_like(pull_weight))

    def window(field):
        for step in range(NSTEP):
            field = advance(field, coefficients)
        return couple(field, mask_plane, pull_cells, put_cells, live_weight)
    linear_state, adjoint = jax.vjp(window, increment)
    gradient = adjoint(linear_state - innovation)[0] + increment
    return (linear_state, gradient)
```

```python
import functools

import jax
import jax.numpy as jnp
from jax import lax
from jax.experimental import pallas as pl
from jax.experimental.pallas import tpu as pltpu
from jax.sharding import PartitionSpec as P

NSTEP = 4
LANES = 128
HALO = 4


def shifted(value, amount, axis):
    return pltpu.roll(value, amount % value.shape[axis], axis)


def coefficients_of(diffusivity, mask):
    half = mask * 0.5
    pairs = ((-1, 1), (1, 1), (1, 0), (-1, 0))
    return [
        half * shifted(mask, by, axis) * (diffusivity + shifted(diffusivity, by, axis))
        for by, axis in pairs
    ]


def stepped(field, coefficients):
    east, west, south, north = coefficients
    change = east * (shifted(field, -1, 1) - field) + west * (shifted(field, 1, 1) - field)
    change = change + south * (shifted(field, 1, 0) - field)
    change = change + north * (shifted(field, -1, 0) - field)
    return field + change


def forward_kernel(height, width, field_ref, extended_ref, state_ref):
    levels = field_ref.shape[0]
    mask = extended_ref[levels]

    def level(at, carry):
        coefficients = coefficients_of(extended_ref[at], mask)
        field = field_ref[at]
        for _ in range(NSTEP):
            field = stepped(field, coefficients)
        state_ref[at] = field[:height, :width]
        return carry

    lax.fori_loop(0, levels, level, 0)


def adjoint_kernel(height, width, field_ref, extended_ref, increment_ref, gradient_ref):
    levels = field_ref.shape[0]
    mask = extended_ref[levels]

    def level(at, carry):
        coefficients = coefficients_of(extended_ref[at], mask)
        field = field_ref[at]
        for _ in range(NSTEP):
            field = stepped(field, coefficients)
        gradient_ref[at] = field[:height, :width] + increment_ref[at]
        return carry

    lax.fori_loop(0, levels, level, 0)


def table_of(plane):
    parts = [plane[:, at : at + LANES] for at in range(0, plane.shape[1], LANES)]
    return jnp.concatenate(parts, axis=0)


def plane_of(table, height):
    parts = [table[at : at + height] for at in range(0, table.shape[0], height)]
    return jnp.concatenate(parts, axis=1)


def split_cell(cell, height, width):
    row = cell // width
    column = cell - row * width
    tile = column // LANES
    return tile * height + row, column - tile * LANES


def looked_up(table_ref, index, high, low):
    rows = table_ref.shape[-2]

    def one(row, found):
        line = jnp.broadcast_to(table_ref[index + (pl.ds(row, 1), slice(None))], low.shape)
        return jnp.where(high == row, jnp.take_along_axis(line, low, axis=1), found)

    found = jnp.zeros(low.shape, jnp.float32)
    for row in range(rows):
        found = one(row, found)
    return found


def spread(values, high, low, rows):
    first = values.astype(jnp.bfloat16).astype(jnp.float32)
    second = values - first
    row_at = lax.broadcasted_iota(jnp.int32, (rows, LANES), 0)
    lane_at = lax.broadcasted_iota(jnp.int32, (LANES, LANES), 0)
    left, right = [], []
    for r in range(values.shape[0]):
        hit = high[r : r + 1] == row_at
        top = jnp.where(hit, first[r : r + 1], 0.0).astype(jnp.bfloat16)
        bottom = jnp.where(hit, second[r : r + 1], 0.0).astype(jnp.bfloat16)
        left.append(jnp.concatenate([top, bottom], axis=0))
        right.append(jnp.where(low[r : r + 1] == lane_at, 1.0, 0.0).astype(jnp.bfloat16))
    return lax.dot_general(
        jnp.concatenate(left, axis=1),
        jnp.concatenate(right, axis=1),
        (((1,), (1,)), ((), ())),
        preferred_element_type=jnp.float32,
    )


def couple_kernel(
    height,
    width,
    count_ref,
    source_ref,
    pull_ref,
    put_ref,
    weight_ref,
    mask_ref,
    state_ref,
    innovation_ref,
    linear_ref,
    adjoint_ref,
    sums_ref,
    total_ref,
    residual_ref,
):
    bands = source_ref.shape[0]
    lines = pull_ref.shape[1]
    rows = height * width // LANES
    deep = min(8, lines)
    block = deep * LANES
    slot = lax.broadcasted_iota(jnp.int32, (deep, LANES), 0) * LANES
    slot = slot + lax.broadcasted_iota(jnp.int32, (deep, LANES), 1)

    def slots(band, at):
        where = pl.ds(pl.multiple_of(at * deep, deep), deep)
        pull = split_cell(pull_ref[band, where, :], height, width)
        put = split_cell(put_ref[band, where, :], height, width)
        live = slot + at * block < count_ref[band]
        return pull, put, jnp.where(live, weight_ref[band, where, :], 0.0)

    def blocks(band):
        return (count_ref[band] + block - 1) // block

    total_ref[...] = jnp.zeros_like(total_ref)

    def forward_band(band, carry):
        def body(at, carry):
            pull, put, weight = slots(band, at)
            values = weight * looked_up(source_ref, (band,), *pull)
            total_ref[...] += spread(values, *put, rows)
            return carry

        return lax.fori_loop(0, blocks(band), body, carry)

    lax.fori_loop(0, bands, forward_band, 0)
    mask = mask_ref[...]
    income = plane_of(total_ref[:rows] + total_ref[rows:], height)
    linear_ref[...] = state_ref[...]
    linear_ref[0] = state_ref[0] + mask * income
    adjoint_ref[...] = linear_ref[...] - innovation_ref[...]
    residual_ref[...] = table_of(mask * adjoint_ref[0])

    def backward_band(band, carry):
        total_ref[...] = jnp.zeros_like(total_ref)

        def body(at, carry):
            pull, put, weight = slots(band, at)
            values = weight * looked_up(residual_ref, (), *put)
            total_ref[...] += spread(values, *pull, rows)
            return carry

        lax.fori_loop(0, blocks(band), body, 0)
        sums_ref[band] = total_ref[:rows] + total_ref[rows:]
        return carry

    lax.fori_loop(0, bands, backward_band, 0)


def over(axis, value, pairs):
    return lax.ppermute(value, axis, pairs)


def extended(cells):
    lons = lax.axis_size("lon")
    lats = lax.axis_size("lat")
    height, width = cells.shape[1:]
    round_up = [(i, (i + 1) % lons) for i in range(lons)]
    round_down = [((i + 1) % lons, i) for i in range(lons)]
    west = over("lon", cells[:, :, width - HALO :], round_up)
    east = over("lon", cells[:, :, :HALO], round_down)
    gap = jnp.zeros(cells.shape[:2] + (LANES - 2 * HALO,), cells.dtype)
    wide = jnp.concatenate([cells, east, gap, west], axis=2)
    up = [(i, i + 1) for i in range(lats - 1)]
    down = [(i + 1, i) for i in range(lats - 1)]
    south = over("lat", wide[:, height - HALO :], up)
    north = over("lat", wide[:, :HALO], down)
    mirror = over("lon", wide[:, height - HALO :], [(i, lons - 1 - i) for i in range(lons)])
    mirror = jnp.roll(mirror[:, ::-1, ::-1], -LANES, axis=2)
    fold = (lax.axis_index("comp") == 1) & (lax.axis_index("lat") == lats - 1)
    return jnp.concatenate([wide, jnp.where(fold, mirror, north), south], axis=1)


def local(
    increment, diffusivity, innovation, land_mask, pull_cells, put_cells, pull_weight, pull_count
):
    levels, height, width = increment.shape[1:]
    bands = lax.axis_size("lat")
    rows = height * width // LANES
    capacity = pull_cells.shape[-1]
    lines = capacity // LANES
    ocean = lax.axis_index("comp") == 1
    mask = jnp.where(ocean, land_mask.astype(jnp.float32), jnp.ones(land_mask.shape, jnp.float32))
    whole = pl.BlockSpec(memory_space=pltpu.VMEM)
    params = pltpu.CompilerParams(vmem_limit_bytes=48 * 1024 * 1024)
    block = jax.ShapeDtypeStruct((levels, height, width), jnp.float32)

    fixed = jnp.concatenate([diffusivity[0], mask[None]], axis=0)
    both = extended(jnp.concatenate([increment[0], fixed], axis=0))
    state = pl.pallas_call(
        functools.partial(forward_kernel, height, width),
        out_shape=block,
        in_specs=[whole, whole],
        out_specs=whole,
        compiler_params=params,
    )(both[:levels], both[levels:])

    surface = table_of(mask * state[0])
    swap = [(0, 1), (1, 0)]
    source = lax.all_gather(over("comp", surface, swap), "lat", axis=0, tiled=False)
    linear, adjoint, sums = pl.pallas_call(
        functools.partial(couple_kernel, height, width),
        out_shape=(block, block, jax.ShapeDtypeStruct((bands, rows, LANES), jnp.float32)),
        in_specs=[pl.BlockSpec(memory_space=pltpu.SMEM)] + [whole] * 7,
        out_specs=(whole, whole, whole),
        scratch_shapes=[
            pltpu.VMEM((2 * rows, LANES), jnp.float32),
            pltpu.VMEM((rows, LANES), jnp.float32),
        ],
        compiler_params=params,
    )(
        pull_count.reshape(bands),
        source,
        pull_cells.reshape(bands, lines, LANES),
        put_cells.reshape(bands, lines, LANES),
        pull_weight.reshape(bands, lines, LANES),
        mask,
        state,
        innovation[0],
    )
    band_sums = lax.psum_scatter(sums, "lat", scatter_dimension=0, tiled=False)
    returned = plane_of(over("comp", band_sums, swap), height)
    adjoint = adjoint.at[0].add(mask * returned)
    gradient = pl.pallas_call(
        functools.partial(adjoint_kernel, height, width),
        out_shape=block,
        in_specs=[whole, whole, whole],
        out_specs=whole,
        compiler_params=params,
    )(extended(adjoint), both[levels:], increment[0])
    return (linear[None], gradient[None])


def solution(mesh):
    placed = (
        P("comp", None, "lat", "lon"),
        P("comp", None, "lat", "lon"),
        P("comp", None, "lat", "lon"),
        P("lat", "lon"),
        P("comp", "lat", "lon", None, None),
        P("comp", "lat", "lon", None, None),
        P("comp", "lat", "lon", None, None),
        P("comp", "lat", "lon", None),
    )
    return jax.shard_map(
        local,
        mesh=mesh,
        in_specs=placed,
        out_specs=(P("comp", None, "lat", "lon"), P("comp", None, "lat", "lon")),
        check_vma=False,
    )
```

```python
import functools

import jax
import jax.numpy as jnp
from jax import lax
from jax.experimental import pallas as pl
from jax.experimental.pallas import tpu as pltpu
from jax.sharding import PartitionSpec as P

NSTEP = 4
LANES = 128
HALO = 4
MESH = pl.DeviceIdType.MESH


def shifted(value, amount, axis):
    return pltpu.roll(value, amount % value.shape[axis], axis)


def coefficients_of(diffusivity, mask):
    half = mask * 0.5
    pairs = ((-1, 1), (1, 1), (1, 0), (-1, 0))
    return [
        half * shifted(mask, by, axis) * (diffusivity + shifted(diffusivity, by, axis))
        for by, axis in pairs
    ]


def stepped(field, coefficients):
    east, west, south, north = coefficients
    change = east * (shifted(field, -1, 1) - field) + west * (shifted(field, 1, 1) - field)
    change = change + south * (shifted(field, 1, 0) - field)
    change = change + north * (shifted(field, -1, 0) - field)
    return field + change


def table_of(plane):
    parts = [plane[:, at : at + LANES] for at in range(0, plane.shape[1], LANES)]
    return jnp.concatenate(parts, axis=0)


def plane_of(table, height):
    parts = [table[at : at + height] for at in range(0, table.shape[0], height)]
    return jnp.concatenate(parts, axis=1)


def split_cell(cell, height, width):
    row = cell // width
    column = cell - row * width
    tile = column // LANES
    return tile * height + row, column - tile * LANES


def looked_up(table_ref, index, high, low):
    rows = table_ref.shape[-2]

    def one(row, found):
        line = jnp.broadcast_to(table_ref[index + (pl.ds(row, 1), slice(None))], low.shape)
        return jnp.where(high == row, jnp.take_along_axis(line, low, axis=1), found)

    found = jnp.zeros(low.shape, jnp.float32)
    for row in range(rows):
        found = one(row, found)
    return found


def spread(values, high, low, rows):
    first = values.astype(jnp.bfloat16).astype(jnp.float32)
    second = values - first
    row_at = lax.broadcasted_iota(jnp.int32, (rows, LANES), 0)
    lane_at = lax.broadcasted_iota(jnp.int32, (LANES, LANES), 0)
    left, right = [], []
    for r in range(values.shape[0]):
        hit = high[r : r + 1] == row_at
        top = jnp.where(hit, first[r : r + 1], 0.0).astype(jnp.bfloat16)
        bottom = jnp.where(hit, second[r : r + 1], 0.0).astype(jnp.bfloat16)
        left.append(jnp.concatenate([top, bottom], axis=0))
        right.append(jnp.where(low[r : r + 1] == lane_at, 1.0, 0.0).astype(jnp.bfloat16))
    return lax.dot_general(
        jnp.concatenate(left, axis=1),
        jnp.concatenate(right, axis=1),
        (((1,), (1,)), ((), ())),
        preferred_element_type=jnp.float32,
    )


def couple_kernel(
    height,
    width,
    count_ref,
    source_ref,
    pull_ref,
    put_ref,
    weight_ref,
    mask_ref,
    state_ref,
    innovation_ref,
    linear_ref,
    adjoint_ref,
    sums_ref,
    total_ref,
    residual_ref,
):
    bands = source_ref.shape[0]
    lines = pull_ref.shape[1]
    rows = height * width // LANES
    deep = min(8, lines)
    block = deep * LANES
    slot = lax.broadcasted_iota(jnp.int32, (deep, LANES), 0) * LANES
    slot = slot + lax.broadcasted_iota(jnp.int32, (deep, LANES), 1)

    def slots(band, at):
        where = pl.ds(pl.multiple_of(at * deep, deep), deep)
        pull = split_cell(pull_ref[band, where, :], height, width)
        put = split_cell(put_ref[band, where, :], height, width)
        live = slot + at * block < count_ref[band]
        return pull, put, jnp.where(live, weight_ref[band, where, :], 0.0)

    def blocks(band):
        return (count_ref[band] + block - 1) // block

    total_ref[...] = jnp.zeros_like(total_ref)

    def forward_band(band, carry):
        def body(at, carry):
            pull, put, weight = slots(band, at)
            values = weight * looked_up(source_ref, (band,), *pull)
            total_ref[...] += spread(values, *put, rows)
            return carry

        return lax.fori_loop(0, blocks(band), body, carry)

    lax.fori_loop(0, bands, forward_band, 0)
    mask = mask_ref[...]
    income = plane_of(total_ref[:rows] + total_ref[rows:], height)
    linear_ref[...] = state_ref[...]
    linear_ref[0] = state_ref[0] + mask * income
    adjoint_ref[...] = linear_ref[...] - innovation_ref[...]
    residual_ref[...] = table_of(mask * adjoint_ref[0])

    def backward_band(band, carry):
        total_ref[...] = jnp.zeros_like(total_ref)

        def body(at, carry):
            pull, put, weight = slots(band, at)
            values = weight * looked_up(residual_ref, (), *put)
            total_ref[...] += spread(values, *pull, rows)
            return carry

        lax.fori_loop(0, blocks(band), body, 0)
        sums_ref[band] = total_ref[:rows] + total_ref[rows:]
        return carry

    lax.fori_loop(0, bands, backward_band, 0)


def place():
    comp, lat, lon = (lax.axis_index(name) for name in ("comp", "lat", "lon"))
    lats, lons = lax.axis_size("lat"), lax.axis_size("lon")
    return comp, lat, lon, lats, lons


def greet(has_south, has_north, at_fold):
    comp, lat, lon, lats, lons = place()
    barrier = pltpu.get_barrier_semaphore()

    def hail(*where):
        pl.semaphore_signal(barrier, inc=1, device_id=where, device_id_type=MESH)

    hail(comp, lat, lax.rem(lon + 1, lons))
    hail(comp, lat, lax.rem(lon + lons - 1, lons))
    pl.when(has_south)(lambda: hail(comp, lat - 1, lon))
    pl.when(has_north)(lambda: hail(comp, lat + 1, lon))
    pl.when(at_fold)(lambda: hail(comp, lat, lons - 1 - lon))

    def across(band, carry):
        hail(1 - comp, band, lon)
        return carry

    lax.fori_loop(0, lats, across, 0)
    rows = has_south.astype(jnp.int32) + has_north.astype(jnp.int32) + at_fold.astype(jnp.int32)
    pl.semaphore_wait(barrier, 2 + lats + rows)


def edges():
    comp, lat, lon, lats, lons = place()
    return lat > 0, lat < lats - 1, (comp == 1) & (lat == lats - 1)


def remote(source, target, sems, where):
    return pltpu.make_async_remote_copy(
        src_ref=source,
        dst_ref=target,
        send_sem=sems[0],
        recv_sem=sems[1],
        device_id=where,
        device_id_type=MESH,
    )


def lon_copies(at, buffers):
    sent, came, sems = buffers
    comp, lat, lon, lats, lons = place()
    ends = (lax.rem(lon + 1, lons), lax.rem(lon + lons - 1, lons))
    return [
        remote(
            sent.at[at, way],
            came.at[at, way],
            (sems.at[0, at, way], sems.at[1, at, way]),
            (comp, lat, ends[way]),
        )
        for way in range(2)
    ]


def lon_pack(sent, at, planes):
    lane = lax.broadcasted_iota(jnp.int32, (planes[0].shape[0], LANES), 1)
    ahead = jnp.zeros(lane.shape, jnp.float32)
    behind = jnp.zeros(lane.shape, jnp.float32)
    for k, plane in enumerate(planes):
        inside = (lane >= HALO * k) & (lane < HALO * (k + 1))
        tail = shifted(plane[:, plane.shape[1] - LANES :], HALO * k + HALO, 1)
        head = shifted(plane[:, :LANES], HALO * k, 1)
        ahead = jnp.where(inside, tail, ahead)
        behind = jnp.where(inside, head, behind)
    sent[at, 0] = ahead
    sent[at, 1] = behind


def lon_unpack(came, at, k):
    west, east = came[at, 0], came[at, 1]
    lane = lax.broadcasted_iota(jnp.int32, west.shape, 1)
    ends = jnp.where(lane >= LANES - HALO, shifted(west, -HALO * (k + 1), 1), 0.0)
    return jnp.where(lane < HALO, shifted(east, -HALO * k, 1), ends)


def mirrored(rows):
    tiles = []
    for at in range(0, rows.shape[1], LANES):
        tile = rows[:, at : at + LANES]
        for axis, bits in ((1, (1, 2, 4, 8, 16, 32, 64)), (0, (1, 2))):
            index = lax.broadcasted_iota(jnp.int32, tile.shape, axis)
            for bit in bits:
                odd = lax.rem(index // bit, 2) == 1
                tile = jnp.where(odd, shifted(tile, bit, axis), shifted(tile, -bit, axis))
        tiles.append(tile)
    own = tiles[-2::-1]
    return jnp.concatenate(own + tiles[-1:], axis=1)


def lat_copies(at, buffers):
    sent, came, sems = buffers
    comp, lat, lon, lats, lons = place()
    has_south, has_north, at_fold = edges()

    def one(way, slot, where):
        return remote(
            sent.at[at, way],
            came.at[at, slot],
            (sems.at[0, at, way], sems.at[1, at, slot]),
            where,
        )

    return (
        (has_north, one(0, 0, (comp, lat + 1, lon))),
        (has_south, one(1, 1, (comp, lat - 1, lon))),
        (at_fold, one(0, 1, (comp, lat, lons - 1 - lon))),
    )


def lat_start(at, buffers):
    for there, copy in lat_copies(at, buffers):
        pl.when(there)(copy.start)


def lat_sent(at, buffers):
    for there, copy in lat_copies(at, buffers):
        pl.when(there)(copy.wait_send)


def lat_came(at, buffers):
    came = buffers[1]
    has_south, has_north, at_fold = edges()
    up, down, fold = (copy for there, copy in lat_copies(at, buffers))
    pl.when(has_south)(up.wait_recv)
    pl.when(has_north)(down.wait_recv)
    pl.when(at_fold)(fold.wait_recv)

    @pl.when(at_fold)
    def _():
        came[at, 1] = mirrored(came[at, 1])

    @pl.when(jnp.logical_not(has_south))
    def _():
        came[at, 0] = jnp.zeros(came.shape[2:], jnp.float32)

    @pl.when(jnp.logical_not(has_north | at_fold))
    def _():
        came[at, 1] = jnp.zeros(came.shape[2:], jnp.float32)

    south, north = came[at, 0], came[at, 1]
    upper = jnp.concatenate([north[:HALO], south[:HALO]], axis=0)
    lower = jnp.concatenate([north[HALO:], south[HALO:]], axis=0)
    return upper, lower


def lat_pack(sent, at, first, second):
    top = first.shape[0] - HALO
    sent[at, 0] = jnp.concatenate([first[top:], second[top:]], axis=0)
    sent[at, 1] = jnp.concatenate([first[:HALO], second[:HALO]], axis=0)


def band_copies(source, came, sems):
    comp, lat, lon, lats, lons = place()

    def one(band):
        return remote(
            source(band), came.at[lat], (sems.at[0, band], sems.at[1, lat]), (1 - comp, band, lon)
        )

    def arrival(band):
        return remote(
            source(band), came.at[band], (sems.at[0, band], sems.at[1, band]), (1 - comp, band, lon)
        )

    def each(act):
        def body(band, carry):
            act(band)
            return carry

        lax.fori_loop(0, lats, body, 0)

    return (
        lambda: each(lambda band: one(band).start()),
        lambda: each(lambda band: arrival(band).wait_recv()),
        lambda: each(lambda band: one(band).wait_send()),
    )


def forward_kernel(
    increment_ref,
    diffusivity_ref,
    land_ref,
    state_ref,
    fixed_ref,
    source_ref,
    field,
    surface,
    surfaces,
    lon_sent,
    lon_came,
    lat_sent_ref,
    lat_came_ref,
    lon_sems,
    lat_sems,
    band_sems,
):
    levels, height, width = increment_ref.shape
    greet(*edges())
    ocean = lax.axis_index("comp") == 1
    mask = jnp.where(ocean, land_ref[...].astype(jnp.float32), 1.0)
    lons = (lon_sent, lon_came, lon_sems)
    lats = (lat_sent_ref, lat_came_ref, lat_sems)
    planes = [increment_ref[k] for k in range(levels)]
    planes = planes + [diffusivity_ref[k] for k in range(levels)] + [mask]
    lon_pack(lon_sent, 0, planes)
    for copy in lon_copies(0, lons):
        copy.start()
    own = pl.ds(0, height), pl.ds(0, width)
    side = pl.ds(0, height), pl.ds(width, LANES)
    fixed_ref[(levels,) + own] = mask

    def fill(k, carry):
        field[(k,) + own] = increment_ref[k]
        fixed_ref[(k,) + own] = diffusivity_ref[k]
        return carry

    lax.fori_loop(0, levels, fill, 0)
    for copy in lon_copies(0, lons):
        copy.wait_recv()
    for k in range(levels):
        field[(k,) + side] = lon_unpack(lon_came, 0, k)
        fixed_ref[(k,) + side] = lon_unpack(lon_came, 0, levels + k)
    fixed_ref[(levels,) + side] = lon_unpack(lon_came, 0, 2 * levels)

    wide_mask = fixed_ref[levels, pl.ds(0, height), :]
    lat_pack(lat_sent_ref, levels, wide_mask, wide_mask)
    lat_start(levels, lats)

    def send(k, carry):
        rows = pl.ds(0, height)
        lat_pack(lat_sent_ref, k, field[k, rows, :], fixed_ref[k, rows, :])
        lat_start(k, lats)
        return carry

    lax.fori_loop(0, levels, send, 0)
    ends = pl.ds(height, 2 * HALO)
    fixed_ref[levels, ends, :] = lat_came(levels, lats)[0]

    def level(k):
        field[k, ends, :], fixed_ref[k, ends, :] = lat_came(k, lats)
        coefficients = coefficients_of(fixed_ref[k], fixed_ref[levels])
        value = field[k]
        for _ in range(NSTEP):
            value = stepped(value, coefficients)
        state_ref[k] = value[:height, :width]

    level(0)
    surface[...] = table_of(mask * state_ref[0])
    start, arrive, finish = band_copies(lambda band: surface, surfaces, band_sems)
    start()

    def rest(k, carry):
        level(k)
        return carry

    lax.fori_loop(1, levels, rest, 0)
    for copy in lon_copies(0, lons):
        copy.wait_send()

    def drain(k, carry):
        lat_sent(k, lats)
        return carry

    lax.fori_loop(0, levels + 1, drain, 0)
    arrive()
    source_ref[...] = surfaces[...]
    finish()


def adjoint_kernel(
    adjoint_ref,
    sums_ref,
    fixed_ref,
    increment_ref,
    gradient_ref,
    field,
    returns,
    lon_sent,
    lon_came,
    lat_sent_ref,
    lat_came_ref,
    lon_sems,
    lat_sems,
    band_sems,
):
    levels, height, width = increment_ref.shape
    pairs = levels // 2
    greet(*edges())
    start, arrive, finish = band_copies(lambda band: sums_ref.at[band], returns, band_sems)
    start()
    lons = (lon_sent, lon_came, lon_sems)
    lats = (lat_sent_ref, lat_came_ref, lat_sems)
    rows = pl.ds(0, height)
    own = rows, pl.ds(0, width)
    side = rows, pl.ds(width, LANES)
    ends = pl.ds(height, 2 * HALO)
    lon_pack(lon_sent, 0, [adjoint_ref[k] for k in range(1, levels)])
    for copy in lon_copies(0, lons):
        copy.start()

    def fill(k, carry):
        field[(k,) + own] = adjoint_ref[k]
        return carry

    lax.fori_loop(1, levels, fill, 0)
    for copy in lon_copies(0, lons):
        copy.wait_recv()
    for k in range(1, levels):
        field[(k,) + side] = lon_unpack(lon_came, 0, k - 1)

    def send(pair, carry):
        first = field[2 * pair - 1, rows, :]
        second = field[jnp.minimum(2 * pair, levels - 1), rows, :]
        lat_pack(lat_sent_ref, pair, first, second)
        lat_start(pair, lats)
        return carry

    lax.fori_loop(1, pairs + 1, send, 0)
    arrive()

    def add(band, total):
        return total + returns[band]

    total = lax.fori_loop(1, returns.shape[0], add, returns[0])
    mask = fixed_ref[(levels,) + own]
    first = adjoint_ref[0] + mask * plane_of(total, height)
    lon_pack(lon_sent, 1, [first])
    for copy in lon_copies(1, lons):
        copy.start()
    field[(0,) + own] = first

    def sweep(k):
        coefficients = coefficients_of(fixed_ref[k], fixed_ref[levels])
        value = field[k]
        for _ in range(NSTEP):
            value = stepped(value, coefficients)
        gradient_ref[k] = value[:height, :width] + increment_ref[k]

    for copy in lon_copies(1, lons):
        copy.wait_recv()
    field[(0,) + side] = lon_unpack(lon_came, 1, 0)
    wide = field[0, rows, :]
    lat_pack(lat_sent_ref, 0, wide, wide)
    lat_start(0, lats)

    def couple_of(pair, carry):
        later = jnp.minimum(2 * pair, levels - 1)
        upper, lower = lat_came(pair, lats)
        field[later, ends, :] = lower
        field[2 * pair - 1, ends, :] = upper
        sweep(2 * pair - 1)
        pl.when(2 * pair < levels)(lambda: sweep(later))
        return carry

    lax.fori_loop(1, pairs + 1, couple_of, 0)
    field[0, ends, :] = lat_came(0, lats)[0]
    sweep(0)
    for at in range(2):
        for copy in lon_copies(at, lons):
            copy.wait_send()

    def drain(k, carry):
        lat_sent(k, lats)
        return carry

    lax.fori_loop(0, pairs + 1, drain, 0)
    finish()


def local(
    increment, diffusivity, innovation, land_mask, pull_cells, put_cells, pull_weight, pull_count
):
    levels, height, width = increment.shape[1:]
    bands = lax.axis_size("lat")
    rows = height * width // LANES
    lines = pull_cells.shape[-1] // LANES
    tall, wide = height + 2 * HALO, width + LANES
    pairs = levels // 2
    ocean = lax.axis_index("comp") == 1
    mask = jnp.where(ocean, land_mask.astype(jnp.float32), jnp.ones(land_mask.shape, jnp.float32))
    whole = pl.BlockSpec(memory_space=pltpu.VMEM)
    space = 48 * 1024 * 1024

    def real(*shape):
        return jax.ShapeDtypeStruct(shape, jnp.float32)

    def room(*shape):
        return pltpu.VMEM(shape, jnp.float32)

    def halos(sides, messages):
        return [
            room(sides, 2, height, LANES),
            room(sides, 2, height, LANES),
            room(messages, 2, 2 * HALO, wide),
            room(messages, 2, 2 * HALO, wide),
            pltpu.SemaphoreType.DMA((2, sides, 2)),
            pltpu.SemaphoreType.DMA((2, messages, 2)),
            pltpu.SemaphoreType.DMA((2, bands)),
        ]

    block = real(levels, height, width)
    state, fixed, source = pl.pallas_call(
        forward_kernel,
        out_shape=(block, real(levels + 1, tall, wide), real(bands, rows, LANES)),
        in_specs=[whole] * 3,
        out_specs=(whole,) * 3,
        scratch_shapes=[room(levels, tall, wide), room(rows, LANES), room(bands, rows, LANES)]
        + halos(1, levels + 1),
        compiler_params=pltpu.CompilerParams(
            vmem_limit_bytes=space, collective_id=0, has_side_effects=True
        ),
    )(increment[0], diffusivity[0], land_mask)

    linear, adjoint, sums = pl.pallas_call(
        functools.partial(couple_kernel, height, width),
        out_shape=(block, block, real(bands, rows, LANES)),
        in_specs=[pl.BlockSpec(memory_space=pltpu.SMEM)] + [whole] * 7,
        out_specs=(whole, whole, whole),
        scratch_shapes=[room(2 * rows, LANES), room(rows, LANES)],
        compiler_params=pltpu.CompilerParams(vmem_limit_bytes=space),
    )(
        pull_count.reshape(bands),
        source,
        pull_cells.reshape(bands, lines, LANES),
        put_cells.reshape(bands, lines, LANES),
        pull_weight.reshape(bands, lines, LANES),
        mask,
        state,
        innovation[0],
    )

    gradient = pl.pallas_call(
        adjoint_kernel,
        out_shape=block,
        in_specs=[whole] * 4,
        out_specs=whole,
        scratch_shapes=[room(levels, tall, wide), room(bands, rows, LANES)]
        + halos(2, pairs + 1),
        compiler_params=pltpu.CompilerParams(
            vmem_limit_bytes=space, collective_id=1, has_side_effects=True
        ),
    )(adjoint, sums, fixed, increment[0])
    return (linear[None], gradient[None])


def solution(mesh):
    placed = (
        P("comp", None, "lat", "lon"),
        P("comp", None, "lat", "lon"),
        P("comp", None, "lat", "lon"),
        P("lat", "lon"),
        P("comp", "lat", "lon", None, None),
        P("comp", "lat", "lon", None, None),
        P("comp", "lat", "lon", None, None),
        P("comp", "lat", "lon", None),
    )
    return jax.shard_map(
        local,
        mesh=mesh,
        in_specs=placed,
        out_specs=(P("comp", None, "lat", "lon"), P("comp", None, "lat", "lon")),
        check_vma=False,
    )
```

```python
import functools

import jax
import jax.numpy as jnp
from jax import lax
from jax.experimental import pallas as pl
from jax.experimental.pallas import tpu as pltpu
from jax.sharding import PartitionSpec as P

NSTEP = 4
LANES = 128
HALO = 4
MESH = pl.DeviceIdType.MESH


def shifted(value, amount, axis):
    return pltpu.roll(value, amount % value.shape[axis], axis)


def coefficients_of(diffusivity, mask):
    half = mask * 0.5
    pairs = ((-1, 1), (1, 1), (1, 0), (-1, 0))
    return [
        half * shifted(mask, by, axis) * (diffusivity + shifted(diffusivity, by, axis))
        for by, axis in pairs
    ]


def stepped(field, coefficients):
    east, west, south, north = coefficients
    change = east * (shifted(field, -1, 1) - field) + west * (shifted(field, 1, 1) - field)
    change = change + south * (shifted(field, 1, 0) - field)
    change = change + north * (shifted(field, -1, 0) - field)
    return field + change


def table_of(plane):
    parts = [plane[:, at : at + LANES] for at in range(0, plane.shape[1], LANES)]
    return jnp.concatenate(parts, axis=0)


def plane_of(table, height):
    parts = [table[at : at + height] for at in range(0, table.shape[0], height)]
    return jnp.concatenate(parts, axis=1)


def split_cell(cell, height, width):
    row = cell // width
    column = cell - row * width
    tile = column // LANES
    return tile * height + row, column - tile * LANES


def looked_up(table_ref, index, high, low):
    rows = table_ref.shape[-2]

    def one(row, found):
        line = jnp.broadcast_to(table_ref[index + (pl.ds(row, 1), slice(None))], low.shape)
        return jnp.where(high == row, jnp.take_along_axis(line, low, axis=1, mode="promise_in_bounds"), found)

    found = jnp.zeros(low.shape, jnp.float32)
    for row in range(rows):
        found = one(row, found)
    return found


def spread(values, high, low, rows):
    narrow = jnp.bfloat16
    pack = 16

    def lined(row, count):
        tile = jnp.broadcast_to(row.astype(jnp.float32), (pack, LANES)).astype(narrow)
        return jnp.concatenate([tile] * (count // pack), axis=0)

    first = values.astype(narrow).astype(jnp.float32)
    second = values - first
    row_at = lax.broadcasted_iota(jnp.int32, (rows, LANES), 0).astype(jnp.float32).astype(narrow)
    lane_at = lax.broadcasted_iota(jnp.int32, (LANES, LANES), 0).astype(jnp.float32).astype(narrow)
    one, zero = jnp.ones((), narrow), jnp.zeros((), narrow)
    left, right = [], []
    for r in range(values.shape[0]):
        hit = lined(high[r : r + 1], rows) == row_at
        top = jnp.where(hit, lined(first[r : r + 1], rows), zero)
        bottom = jnp.where(hit, lined(second[r : r + 1], rows), zero)
        left.append(jnp.concatenate([top, bottom], axis=0))
        right.append(jnp.where(lined(low[r : r + 1], LANES) == lane_at, one, zero))
    return lax.dot_general(
        jnp.concatenate(left, axis=1),
        jnp.concatenate(right, axis=1),
        (((1,), (1,)), ((), ())),
        preferred_element_type=jnp.float32,
    )


def couple_kernel(
    height,
    width,
    count_ref,
    source_ref,
    pull_ref,
    put_ref,
    weight_ref,
    land_ref,
    state_ref,
    innovation_ref,
    linear_ref,
    adjoint_ref,
    sums_ref,
    total_ref,
    residual_ref,
):
    bands = source_ref.shape[0]
    lines = pull_ref.shape[1]
    rows = height * width // LANES
    deep = min(16, lines)
    block = deep * LANES
    slot = lax.broadcasted_iota(jnp.int32, (deep, LANES), 0) * LANES
    slot = slot + lax.broadcasted_iota(jnp.int32, (deep, LANES), 1)

    def slots(band, at):
        where = pl.ds(pl.multiple_of(at * deep, deep), deep)
        pull = split_cell(pull_ref[band, where, :], height, width)
        put = split_cell(put_ref[band, where, :], height, width)
        live = slot + at * block < count_ref[band]
        return pull, put, jnp.where(live, weight_ref[band, where, :], 0.0)

    def blocks(band):
        return (count_ref[band] + block - 1) // block

    total_ref[...] = jnp.zeros_like(total_ref)

    def forward_band(band, carry):
        def body(at, carry):
            pull, put, weight = slots(band, at)
            values = weight * looked_up(source_ref, (band,), *pull)
            total_ref[...] += spread(values, *put, rows)
            return carry

        return lax.fori_loop(0, blocks(band), body, carry)

    lax.fori_loop(0, bands, forward_band, 0)
    ocean = lax.axis_index("comp") == 1
    mask = jnp.where(ocean, land_ref[...].astype(jnp.float32), 1.0)
    income = plane_of(total_ref[:rows] + total_ref[rows:], height)
    linear_ref[...] = state_ref[...]
    linear_ref[0] = state_ref[0] + mask * income
    adjoint_ref[...] = linear_ref[...] - innovation_ref[...]
    residual_ref[...] = table_of(mask * adjoint_ref[0])

    def backward_band(band, carry):
        total_ref[...] = jnp.zeros_like(total_ref)

        def body(at, carry):
            pull, put, weight = slots(band, at)
            values = weight * looked_up(residual_ref, (), *put)
            total_ref[...] += spread(values, *pull, rows)
            return carry

        lax.fori_loop(0, blocks(band), body, 0)
        sums_ref[band] = total_ref[:rows] + total_ref[rows:]
        return carry

    lax.fori_loop(0, bands, backward_band, 0)


def place():
    comp, lat, lon = (lax.axis_index(name) for name in ("comp", "lat", "lon"))
    lats, lons = lax.axis_size("lat"), lax.axis_size("lon")
    return comp, lat, lon, lats, lons


def greet(has_south, has_north, at_fold):
    comp, lat, lon, lats, lons = place()
    barrier = pltpu.get_barrier_semaphore()

    def hail(*where):
        pl.semaphore_signal(barrier, inc=1, device_id=where, device_id_type=MESH)

    hail(comp, lat, lax.rem(lon + 1, lons))
    hail(comp, lat, lax.rem(lon + lons - 1, lons))
    pl.when(has_south)(lambda: hail(comp, lat - 1, lon))
    pl.when(has_north)(lambda: hail(comp, lat + 1, lon))
    pl.when(at_fold)(lambda: hail(comp, lat, lons - 1 - lon))

    def across(band, carry):
        hail(1 - comp, band, lon)
        return carry

    lax.fori_loop(0, lats, across, 0)
    rows = has_south.astype(jnp.int32) + has_north.astype(jnp.int32) + at_fold.astype(jnp.int32)
    pl.semaphore_wait(barrier, 2 + lats + rows)


def edges():
    comp, lat, lon, lats, lons = place()
    return lat > 0, lat < lats - 1, (comp == 1) & (lat == lats - 1)


def remote(source, target, sems, where):
    return pltpu.make_async_remote_copy(
        src_ref=source,
        dst_ref=target,
        send_sem=sems[0],
        recv_sem=sems[1],
        device_id=where,
        device_id_type=MESH,
    )


def lon_copies(at, buffers):
    sent, came, sems = buffers
    comp, lat, lon, lats, lons = place()
    ends = (lax.rem(lon + 1, lons), lax.rem(lon + lons - 1, lons))
    return [
        remote(
            sent.at[at, way],
            came.at[at, way],
            (sems.at[0, at, way], sems.at[1, at, way]),
            (comp, lat, ends[way]),
        )
        for way in range(2)
    ]


def lon_pack(sent, at, planes):
    lane = lax.broadcasted_iota(jnp.int32, (planes[0].shape[0], LANES), 1)
    ahead = jnp.zeros(lane.shape, jnp.float32)
    behind = jnp.zeros(lane.shape, jnp.float32)
    for k, plane in enumerate(planes):
        inside = (lane >= HALO * k) & (lane < HALO * (k + 1))
        tail = shifted(plane[:, plane.shape[1] - LANES :], HALO * k + HALO, 1)
        head = shifted(plane[:, :LANES], HALO * k, 1)
        ahead = jnp.where(inside, tail, ahead)
        behind = jnp.where(inside, head, behind)
    sent[at, 0] = ahead
    sent[at, 1] = behind


def lon_unpack(came, at, k):
    west, east = came[at, 0], came[at, 1]
    lane = lax.broadcasted_iota(jnp.int32, west.shape, 1)
    ends = jnp.where(lane >= LANES - HALO, shifted(west, -HALO * (k + 1), 1), 0.0)
    return jnp.where(lane < HALO, shifted(east, -HALO * k, 1), ends)


def mirrored(rows):
    tiles = []
    for at in range(0, rows.shape[1], LANES):
        tile = rows[:, at : at + LANES]
        for axis, bits in ((1, (1, 2, 4, 8, 16, 32, 64)), (0, (1, 2))):
            index = lax.broadcasted_iota(jnp.int32, tile.shape, axis)
            for bit in bits:
                odd = lax.rem(index // bit, 2) == 1
                tile = jnp.where(odd, shifted(tile, bit, axis), shifted(tile, -bit, axis))
        tiles.append(tile)
    own = tiles[-2::-1]
    return jnp.concatenate(own + tiles[-1:], axis=1)


def lat_copies(at, buffers):
    sent, came, sems = buffers
    comp, lat, lon, lats, lons = place()
    has_south, has_north, at_fold = edges()

    def one(way, slot, where):
        return remote(
            sent.at[at, way],
            came.at[at, slot],
            (sems.at[0, at, way], sems.at[1, at, slot]),
            where,
        )

    return (
        (has_north, one(0, 0, (comp, lat + 1, lon))),
        (has_south, one(1, 1, (comp, lat - 1, lon))),
        (at_fold, one(0, 1, (comp, lat, lons - 1 - lon))),
    )


def lat_start(at, buffers):
    for there, copy in lat_copies(at, buffers):
        pl.when(there)(copy.start)


def lat_sent(at, buffers):
    for there, copy in lat_copies(at, buffers):
        pl.when(there)(copy.wait_send)


def lat_came(at, buffers):
    came = buffers[1]
    has_south, has_north, at_fold = edges()
    up, down, fold = (copy for there, copy in lat_copies(at, buffers))
    pl.when(has_south)(up.wait_recv)
    pl.when(has_north)(down.wait_recv)
    pl.when(at_fold)(fold.wait_recv)

    @pl.when(at_fold)
    def _():
        came[at, 1] = mirrored(came[at, 1])

    @pl.when(jnp.logical_not(has_south))
    def _():
        came[at, 0] = jnp.zeros(came.shape[2:], jnp.float32)

    @pl.when(jnp.logical_not(has_north | at_fold))
    def _():
        came[at, 1] = jnp.zeros(came.shape[2:], jnp.float32)

    south, north = came[at, 0], came[at, 1]
    upper = jnp.concatenate([north[:HALO], south[:HALO]], axis=0)
    lower = jnp.concatenate([north[HALO:], south[HALO:]], axis=0)
    return upper, lower


def lat_pack(sent, at, first, second):
    top = first.shape[0] - HALO
    sent[at, 0] = jnp.concatenate([first[top:], second[top:]], axis=0)
    sent[at, 1] = jnp.concatenate([first[:HALO], second[:HALO]], axis=0)


def band_copies(source, came, sems):
    comp, lat, lon, lats, lons = place()

    def one(band):
        return remote(
            source(band), came.at[lat], (sems.at[0, band], sems.at[1, lat]), (1 - comp, band, lon)
        )

    def arrival(band):
        return remote(
            source(band), came.at[band], (sems.at[0, band], sems.at[1, band]), (1 - comp, band, lon)
        )

    def each(act):
        def body(band, carry):
            act(band)
            return carry

        lax.fori_loop(0, lats, body, 0)

    return (
        lambda: each(lambda band: one(band).start()),
        lambda: each(lambda band: arrival(band).wait_recv()),
        lambda: each(lambda band: one(band).wait_send()),
    )


def forward_kernel(
    increment_ref,
    diffusivity_ref,
    land_ref,
    state_ref,
    fixed_ref,
    source_ref,
    field,
    surface,
    surfaces,
    lon_sent,
    lon_came,
    lat_sent_ref,
    lat_came_ref,
    lon_sems,
    lat_sems,
    band_sems,
):
    levels, height, width = increment_ref.shape
    greet(*edges())
    ocean = lax.axis_index("comp") == 1
    mask = jnp.where(ocean, land_ref[...].astype(jnp.float32), 1.0)
    lons = (lon_sent, lon_came, lon_sems)
    lats = (lat_sent_ref, lat_came_ref, lat_sems)
    planes = [increment_ref[k] for k in range(levels)]
    planes = planes + [diffusivity_ref[k] for k in range(levels)] + [mask]
    lon_pack(lon_sent, 0, planes)
    for copy in lon_copies(0, lons):
        copy.start()
    own = pl.ds(0, height), pl.ds(0, width)
    side = pl.ds(0, height), pl.ds(width, LANES)
    fixed_ref[(levels,) + own] = mask

    def fill(k, carry):
        field[(k,) + own] = increment_ref[k]
        fixed_ref[(k,) + own] = diffusivity_ref[k]
        return carry

    lax.fori_loop(0, levels, fill, 0)
    for copy in lon_copies(0, lons):
        copy.wait_recv()
    for k in range(levels):
        field[(k,) + side] = lon_unpack(lon_came, 0, k)
        fixed_ref[(k,) + side] = lon_unpack(lon_came, 0, levels + k)
    fixed_ref[(levels,) + side] = lon_unpack(lon_came, 0, 2 * levels)

    wide_mask = fixed_ref[levels, pl.ds(0, height), :]
    lat_pack(lat_sent_ref, levels, wide_mask, wide_mask)
    lat_start(levels, lats)

    def send(k, carry):
        rows = pl.ds(0, height)
        lat_pack(lat_sent_ref, k, field[k, rows, :], fixed_ref[k, rows, :])
        lat_start(k, lats)
        return carry

    lax.fori_loop(0, levels, send, 0)
    ends = pl.ds(height, 2 * HALO)
    fixed_ref[levels, ends, :] = lat_came(levels, lats)[0]

    def level(k):
        field[k, ends, :], fixed_ref[k, ends, :] = lat_came(k, lats)
        coefficients = coefficients_of(fixed_ref[k], fixed_ref[levels])
        value = field[k]
        for _ in range(NSTEP):
            value = stepped(value, coefficients)
        state_ref[k] = value[:height, :width]

    level(0)
    surface[...] = table_of(mask * state_ref[0])
    start, arrive, finish = band_copies(lambda band: surface, surfaces, band_sems)
    start()

    def rest(k, carry):
        level(k)
        return carry

    lax.fori_loop(1, levels, rest, 0)
    for copy in lon_copies(0, lons):
        copy.wait_send()

    def drain(k, carry):
        lat_sent(k, lats)
        return carry

    lax.fori_loop(0, levels + 1, drain, 0)
    arrive()
    source_ref[...] = surfaces[...]
    finish()


def adjoint_kernel(
    adjoint_ref,
    sums_ref,
    fixed_ref,
    increment_ref,
    gradient_ref,
    field,
    returns,
    lon_sent,
    lon_came,
    lat_sent_ref,
    lat_came_ref,
    lon_sems,
    lat_sems,
    band_sems,
):
    levels, height, width = increment_ref.shape
    pairs = levels // 2
    greet(*edges())
    start, arrive, finish = band_copies(lambda band: sums_ref.at[band], returns, band_sems)
    start()
    lons = (lon_sent, lon_came, lon_sems)
    lats = (lat_sent_ref, lat_came_ref, lat_sems)
    rows = pl.ds(0, height)
    own = rows, pl.ds(0, width)
    side = rows, pl.ds(width, LANES)
    ends = pl.ds(height, 2 * HALO)
    lon_pack(lon_sent, 0, [adjoint_ref[k] for k in range(1, levels)])
    for copy in lon_copies(0, lons):
        copy.start()

    def fill(k, carry):
        field[(k,) + own] = adjoint_ref[k]
        return carry

    lax.fori_loop(1, levels, fill, 0)
    for copy in lon_copies(0, lons):
        copy.wait_recv()
    for k in range(1, levels):
        field[(k,) + side] = lon_unpack(lon_came, 0, k - 1)

    def send(pair, carry):
        first = field[2 * pair - 1, rows, :]
        second = field[jnp.minimum(2 * pair, levels - 1), rows, :]
        lat_pack(lat_sent_ref, pair, first, second)
        lat_start(pair, lats)
        return carry

    lax.fori_loop(1, pairs + 1, send, 0)
    arrive()

    def add(band, total):
        return total + returns[band]

    total = lax.fori_loop(1, returns.shape[0], add, returns[0])
    mask = fixed_ref[(levels,) + own]
    first = adjoint_ref[0] + mask * plane_of(total, height)
    lon_pack(lon_sent, 1, [first])
    for copy in lon_copies(1, lons):
        copy.start()
    field[(0,) + own] = first

    def sweep(k):
        coefficients = coefficients_of(fixed_ref[k], fixed_ref[levels])
        value = field[k]
        for _ in range(NSTEP):
            value = stepped(value, coefficients)
        gradient_ref[k] = value[:height, :width] + increment_ref[k]

    for copy in lon_copies(1, lons):
        copy.wait_recv()
    field[(0,) + side] = lon_unpack(lon_came, 1, 0)
    wide = field[0, rows, :]
    lat_pack(lat_sent_ref, 0, wide, wide)
    lat_start(0, lats)

    def couple_of(pair, carry):
        later = jnp.minimum(2 * pair, levels - 1)
        upper, lower = lat_came(pair, lats)
        field[later, ends, :] = lower
        field[2 * pair - 1, ends, :] = upper
        sweep(2 * pair - 1)
        pl.when(2 * pair < levels)(lambda: sweep(later))
        return carry

    lax.fori_loop(1, pairs + 1, couple_of, 0)
    field[0, ends, :] = lat_came(0, lats)[0]
    sweep(0)
    for at in range(2):
        for copy in lon_copies(at, lons):
            copy.wait_send()

    def drain(k, carry):
        lat_sent(k, lats)
        return carry

    lax.fori_loop(0, pairs + 1, drain, 0)
    finish()


def local(
    increment, diffusivity, innovation, land_mask, pull_cells, put_cells, pull_weight, pull_count
):
    levels, height, width = increment.shape[1:]
    bands = lax.axis_size("lat")
    rows = height * width // LANES
    lines = pull_cells.shape[-1] // LANES
    tall, wide = height + 2 * HALO, width + LANES
    pairs = levels // 2
    whole = pl.BlockSpec(memory_space=pltpu.VMEM)
    space = 48 * 1024 * 1024

    def real(*shape):
        return jax.ShapeDtypeStruct(shape, jnp.float32)

    def room(*shape):
        return pltpu.VMEM(shape, jnp.float32)

    def halos(sides, messages):
        return [
            room(sides, 2, height, LANES),
            room(sides, 2, height, LANES),
            room(messages, 2, 2 * HALO, wide),
            room(messages, 2, 2 * HALO, wide),
            pltpu.SemaphoreType.DMA((2, sides, 2)),
            pltpu.SemaphoreType.DMA((2, messages, 2)),
            pltpu.SemaphoreType.DMA((2, bands)),
        ]

    block = real(levels, height, width)
    state, fixed, source = pl.pallas_call(
        forward_kernel,
        out_shape=(block, real(levels + 1, tall, wide), real(bands, rows, LANES)),
        in_specs=[whole] * 3,
        out_specs=(whole,) * 3,
        scratch_shapes=[room(levels, tall, wide), room(rows, LANES), room(bands, rows, LANES)]
        + halos(1, levels + 1),
        compiler_params=pltpu.CompilerParams(
            vmem_limit_bytes=space, collective_id=0, has_side_effects=True
        ),
    )(increment[0], diffusivity[0], land_mask)

    linear, adjoint, sums = pl.pallas_call(
        functools.partial(couple_kernel, height, width),
        out_shape=(block, block, real(bands, rows, LANES)),
        in_specs=[pl.BlockSpec(memory_space=pltpu.SMEM)] + [whole] * 7,
        out_specs=(whole, whole, whole),
        scratch_shapes=[room(2 * rows, LANES), room(rows, LANES)],
        compiler_params=pltpu.CompilerParams(vmem_limit_bytes=space),
    )(
        pull_count.reshape(bands),
        source,
        pull_cells.reshape(bands, lines, LANES),
        put_cells.reshape(bands, lines, LANES),
        pull_weight.reshape(bands, lines, LANES),
        land_mask,
        state,
        innovation[0],
    )

    gradient = pl.pallas_call(
        adjoint_kernel,
        out_shape=block,
        in_specs=[whole] * 4,
        out_specs=whole,
        scratch_shapes=[room(levels, tall, wide), room(bands, rows, LANES)]
        + halos(2, pairs + 1),
        compiler_params=pltpu.CompilerParams(
            vmem_limit_bytes=space, collective_id=1, has_side_effects=True
        ),
    )(adjoint, sums, fixed, increment[0])
    return (linear[None], gradient[None])


def solution(mesh):
    placed = (
        P("comp", None, "lat", "lon"),
        P("comp", None, "lat", "lon"),
        P("comp", None, "lat", "lon"),
        P("lat", "lon"),
        P("comp", "lat", "lon", None, None),
        P("comp", "lat", "lon", None, None),
        P("comp", "lat", "lon", None, None),
        P("comp", "lat", "lon", None),
    )
    return jax.shard_map(
        local,
        mesh=mesh,
        in_specs=placed,
        out_specs=(P("comp", None, "lat", "lon"), P("comp", None, "lat", "lon")),
        check_vma=False,
    )
```

```python
import functools

import jax
import jax.numpy as jnp
from jax import lax
from jax.experimental import pallas as pl
from jax.experimental.pallas import tpu as pltpu
from jax.sharding import PartitionSpec as P

NSTEP = 4
LANES = 128
HALO = 4
MESH = pl.DeviceIdType.MESH


def shifted(value, amount, axis):
    return pltpu.roll(value, amount % value.shape[axis], axis)


def coefficients_of(diffusivity, mask):
    half = mask * 0.5
    pairs = ((-1, 1), (1, 1), (1, 0), (-1, 0))
    return [
        half * shifted(mask, by, axis) * (diffusivity + shifted(diffusivity, by, axis))
        for by, axis in pairs
    ]


def stepped(field, coefficients):
    east, west, south, north = coefficients
    change = east * (shifted(field, -1, 1) - field) + west * (shifted(field, 1, 1) - field)
    change = change + south * (shifted(field, 1, 0) - field)
    change = change + north * (shifted(field, -1, 0) - field)
    return field + change


def table_of(plane):
    parts = [plane[:, at : at + LANES] for at in range(0, plane.shape[1], LANES)]
    return jnp.concatenate(parts, axis=0)


def plane_of(table, height):
    parts = [table[at : at + height] for at in range(0, table.shape[0], height)]
    return jnp.concatenate(parts, axis=1)


def split_cell(cell, height, width):
    row = cell // width
    column = cell - row * width
    tile = column // LANES
    return tile * height + row, column - tile * LANES


def looked_up(table_ref, index, high, low):
    rows = table_ref.shape[-2]

    def one(row, found):
        line = jnp.broadcast_to(table_ref[index + (pl.ds(row, 1), slice(None))], low.shape)
        return jnp.where(high == row, jnp.take_along_axis(line, low, axis=1, mode="promise_in_bounds"), found)

    found = jnp.zeros(low.shape, jnp.float32)
    for row in range(rows):
        found = one(row, found)
    return found


def spread(values, high, low, rows):
    narrow = jnp.bfloat16
    pack = 16

    def lined(row, count):
        tile = jnp.broadcast_to(row.astype(jnp.float32), (pack, LANES)).astype(narrow)
        return jnp.concatenate([tile] * (count // pack), axis=0)

    first = values.astype(narrow).astype(jnp.float32)
    second = values - first
    row_at = lax.broadcasted_iota(jnp.int32, (rows, LANES), 0).astype(jnp.float32).astype(narrow)
    lane_at = lax.broadcasted_iota(jnp.int32, (LANES, LANES), 0).astype(jnp.float32).astype(narrow)
    one, zero = jnp.ones((), narrow), jnp.zeros((), narrow)
    left, right = [], []
    for r in range(values.shape[0]):
        hit = lined(high[r : r + 1], rows) == row_at
        top = jnp.where(hit, lined(first[r : r + 1], rows), zero)
        bottom = jnp.where(hit, lined(second[r : r + 1], rows), zero)
        left.append(jnp.concatenate([top, bottom], axis=0))
        right.append(jnp.where(lined(low[r : r + 1], LANES) == lane_at, one, zero))
    return lax.dot_general(
        jnp.concatenate(left, axis=1),
        jnp.concatenate(right, axis=1),
        (((1,), (1,)), ((), ())),
        preferred_element_type=jnp.float32,
    )


def couple_kernel(
    height,
    width,
    count_ref,
    source_ref,
    pull_ref,
    put_ref,
    weight_ref,
    land_ref,
    state_ref,
    innovation_ref,
    linear_ref,
    adjoint_ref,
    sums_ref,
    total_ref,
    residual_ref,
):
    bands = source_ref.shape[0]
    lines = pull_ref.shape[1]
    rows = height * width // LANES
    deep = min(16, lines)
    block = deep * LANES
    slot = lax.broadcasted_iota(jnp.int32, (deep, LANES), 0) * LANES
    slot = slot + lax.broadcasted_iota(jnp.int32, (deep, LANES), 1)

    def slots(band, at):
        where = pl.ds(pl.multiple_of(at * deep, deep), deep)
        pull = split_cell(pull_ref[band, where, :], height, width)
        put = split_cell(put_ref[band, where, :], height, width)
        live = slot + at * block < count_ref[0, 0, 0, band]
        return pull, put, jnp.where(live, weight_ref[band, where, :], 0.0)

    def blocks(band):
        return (count_ref[0, 0, 0, band] + block - 1) // block

    total_ref[...] = jnp.zeros_like(total_ref)

    def forward_band(band, carry):
        def body(at, carry):
            pull, put, weight = slots(band, at)
            values = weight * looked_up(source_ref, (band,), *pull)
            total_ref[...] += spread(values, *put, rows)
            return carry

        return lax.fori_loop(0, blocks(band), body, carry)

    lax.fori_loop(0, bands, forward_band, 0)
    ocean = lax.axis_index("comp") == 1
    mask = jnp.where(ocean, land_ref[...].astype(jnp.float32), 1.0)
    income = plane_of(total_ref[:rows] + total_ref[rows:], height)
    linear_ref[...] = state_ref[...]
    linear_ref[0] = state_ref[0] + mask * income
    adjoint_ref[...] = linear_ref[...] - innovation_ref[...]
    residual_ref[...] = table_of(mask * adjoint_ref[0])

    def backward_band(band, carry):
        total_ref[...] = jnp.zeros_like(total_ref)

        def body(at, carry):
            pull, put, weight = slots(band, at)
            values = weight * looked_up(residual_ref, (), *put)
            total_ref[...] += spread(values, *pull, rows)
            return carry

        lax.fori_loop(0, blocks(band), body, 0)
        sums_ref[band] = total_ref[:rows] + total_ref[rows:]
        return carry

    lax.fori_loop(0, bands, backward_band, 0)


def place():
    comp, lat, lon = (lax.axis_index(name) for name in ("comp", "lat", "lon"))
    lats, lons = lax.axis_size("lat"), lax.axis_size("lon")
    return comp, lat, lon, lats, lons


def greet(has_south, has_north, at_fold):
    comp, lat, lon, lats, lons = place()
    barrier = pltpu.get_barrier_semaphore()

    def hail(*where):
        pl.semaphore_signal(barrier, inc=1, device_id=where, device_id_type=MESH)

    hail(comp, lat, lax.rem(lon + 1, lons))
    hail(comp, lat, lax.rem(lon + lons - 1, lons))
    pl.when(has_south)(lambda: hail(comp, lat - 1, lon))
    pl.when(has_north)(lambda: hail(comp, lat + 1, lon))
    pl.when(at_fold)(lambda: hail(comp, lat, lons - 1 - lon))

    def across(band, carry):
        hail(1 - comp, band, lon)
        return carry

    lax.fori_loop(0, lats, across, 0)
    rows = has_south.astype(jnp.int32) + has_north.astype(jnp.int32) + at_fold.astype(jnp.int32)
    pl.semaphore_wait(barrier, 2 + lats + rows)


def edges():
    comp, lat, lon, lats, lons = place()
    return lat > 0, lat < lats - 1, (comp == 1) & (lat == lats - 1)


def remote(source, target, sems, where):
    return pltpu.make_async_remote_copy(
        src_ref=source,
        dst_ref=target,
        send_sem=sems[0],
        recv_sem=sems[1],
        device_id=where,
        device_id_type=MESH,
    )


def lon_copies(at, buffers):
    sent, came, sems = buffers
    comp, lat, lon, lats, lons = place()
    ends = (lax.rem(lon + 1, lons), lax.rem(lon + lons - 1, lons))
    return [
        remote(
            sent.at[at, way],
            came.at[at, way],
            (sems.at[0, at, way], sems.at[1, at, way]),
            (comp, lat, ends[way]),
        )
        for way in range(2)
    ]


def lon_pack(sent, at, planes):
    lane = lax.broadcasted_iota(jnp.int32, (planes[0].shape[0], LANES), 1)
    ahead = jnp.zeros(lane.shape, jnp.float32)
    behind = jnp.zeros(lane.shape, jnp.float32)
    for k, plane in enumerate(planes):
        inside = (lane >= HALO * k) & (lane < HALO * (k + 1))
        tail = shifted(plane[:, plane.shape[1] - LANES :], HALO * k + HALO, 1)
        head = shifted(plane[:, :LANES], HALO * k, 1)
        ahead = jnp.where(inside, tail, ahead)
        behind = jnp.where(inside, head, behind)
    sent[at, 0] = ahead
    sent[at, 1] = behind


def lon_unpack(came, at, k):
    west, east = came[at, 0], came[at, 1]
    lane = lax.broadcasted_iota(jnp.int32, west.shape, 1)
    ends = jnp.where(lane >= LANES - HALO, shifted(west, -HALO * (k + 1), 1), 0.0)
    return jnp.where(lane < HALO, shifted(east, -HALO * k, 1), ends)


def mirrored(rows):
    tiles = []
    for at in range(0, rows.shape[1], LANES):
        tile = rows[:, at : at + LANES]
        for axis, bits in ((1, (1, 2, 4, 8, 16, 32, 64)), (0, (1, 2))):
            index = lax.broadcasted_iota(jnp.int32, tile.shape, axis)
            for bit in bits:
                odd = lax.rem(index // bit, 2) == 1
                tile = jnp.where(odd, shifted(tile, bit, axis), shifted(tile, -bit, axis))
        tiles.append(tile)
    own = tiles[-2::-1]
    return jnp.concatenate(own + tiles[-1:], axis=1)


def lat_copies(at, buffers):
    sent, came, sems = buffers
    comp, lat, lon, lats, lons = place()
    has_south, has_north, at_fold = edges()

    def one(way, slot, where):
        return remote(
            sent.at[at, way],
            came.at[at, slot],
            (sems.at[0, at, way], sems.at[1, at, slot]),
            where,
        )

    return (
        (has_north, one(0, 0, (comp, lat + 1, lon))),
        (has_south, one(1, 1, (comp, lat - 1, lon))),
        (at_fold, one(0, 1, (comp, lat, lons - 1 - lon))),
    )


def lat_start(at, buffers):
    for there, copy in lat_copies(at, buffers):
        pl.when(there)(copy.start)


def lat_sent(at, buffers):
    for there, copy in lat_copies(at, buffers):
        pl.when(there)(copy.wait_send)


def lat_came(at, buffers):
    came = buffers[1]
    has_south, has_north, at_fold = edges()
    up, down, fold = (copy for there, copy in lat_copies(at, buffers))
    pl.when(has_south)(up.wait_recv)
    pl.when(has_north)(down.wait_recv)
    pl.when(at_fold)(fold.wait_recv)

    @pl.when(at_fold)
    def _():
        came[at, 1] = mirrored(came[at, 1])

    @pl.when(jnp.logical_not(has_south))
    def _():
        came[at, 0] = jnp.zeros(came.shape[2:], jnp.float32)

    @pl.when(jnp.logical_not(has_north | at_fold))
    def _():
        came[at, 1] = jnp.zeros(came.shape[2:], jnp.float32)

    south, north = came[at, 0], came[at, 1]
    upper = jnp.concatenate([north[:HALO], south[:HALO]], axis=0)
    lower = jnp.concatenate([north[HALO:], south[HALO:]], axis=0)
    return upper, lower


def lat_pack(sent, at, first, second):
    top = first.shape[0] - HALO
    sent[at, 0] = jnp.concatenate([first[top:], second[top:]], axis=0)
    sent[at, 1] = jnp.concatenate([first[:HALO], second[:HALO]], axis=0)


def band_copies(source, came, sems):
    comp, lat, lon, lats, lons = place()

    def one(band):
        return remote(
            source(band), came.at[lat], (sems.at[0, band], sems.at[1, lat]), (1 - comp, band, lon)
        )

    def arrival(band):
        return remote(
            source(band), came.at[band], (sems.at[0, band], sems.at[1, band]), (1 - comp, band, lon)
        )

    def each(act):
        def body(band, carry):
            act(band)
            return carry

        lax.fori_loop(0, lats, body, 0)

    return (
        lambda: each(lambda band: one(band).start()),
        lambda: each(lambda band: arrival(band).wait_recv()),
        lambda: each(lambda band: one(band).wait_send()),
    )


def forward_kernel(
    increment_ref,
    diffusivity_ref,
    land_ref,
    pull_ref,
    put_ref,
    weight_ref,
    state_ref,
    fixed_ref,
    source_ref,
    pull_lines,
    put_lines,
    weight_lines,
    field,
    surface,
    surfaces,
    lon_sent,
    lon_came,
    lat_sent_ref,
    lat_came_ref,
    lon_sems,
    lat_sems,
    band_sems,
):
    levels, height, width = increment_ref.shape
    greet(*edges())
    ocean = lax.axis_index("comp") == 1
    mask = jnp.where(ocean, land_ref[...].astype(jnp.float32), 1.0)
    lons = (lon_sent, lon_came, lon_sems)
    lats = (lat_sent_ref, lat_came_ref, lat_sems)
    planes = [increment_ref[k] for k in range(levels)]
    planes = planes + [diffusivity_ref[k] for k in range(levels)] + [mask]
    lon_pack(lon_sent, 0, planes)
    for copy in lon_copies(0, lons):
        copy.start()
    own = pl.ds(0, height), pl.ds(0, width)
    side = pl.ds(0, height), pl.ds(width, LANES)
    fixed_ref[(levels,) + own] = mask

    def fill(k, carry):
        field[(k,) + own] = increment_ref[k]
        fixed_ref[(k,) + own] = diffusivity_ref[k]
        return carry

    lax.fori_loop(0, levels, fill, 0)
    for line in range(pull_lines.shape[1]):
        lanes = pl.ds(line * LANES, LANES)
        pull_lines[:, line, :] = pull_ref[:, lanes]
        put_lines[:, line, :] = put_ref[:, lanes]
        weight_lines[:, line, :] = weight_ref[:, lanes]
    for copy in lon_copies(0, lons):
        copy.wait_recv()
    for k in range(levels):
        field[(k,) + side] = lon_unpack(lon_came, 0, k)
        fixed_ref[(k,) + side] = lon_unpack(lon_came, 0, levels + k)
    fixed_ref[(levels,) + side] = lon_unpack(lon_came, 0, 2 * levels)

    wide_mask = fixed_ref[levels, pl.ds(0, height), :]
    lat_pack(lat_sent_ref, levels, wide_mask, wide_mask)
    lat_start(levels, lats)

    def send(k, carry):
        rows = pl.ds(0, height)
        lat_pack(lat_sent_ref, k, field[k, rows, :], fixed_ref[k, rows, :])
        lat_start(k, lats)
        return carry

    lax.fori_loop(0, levels, send, 0)
    ends = pl.ds(height, 2 * HALO)
    fixed_ref[levels, ends, :] = lat_came(levels, lats)[0]

    def level(k):
        field[k, ends, :], fixed_ref[k, ends, :] = lat_came(k, lats)
        coefficients = coefficients_of(fixed_ref[k], fixed_ref[levels])
        value = field[k]
        for _ in range(NSTEP):
            value = stepped(value, coefficients)
        state_ref[k] = value[:height, :width]

    level(0)
    surface[...] = table_of(mask * state_ref[0])
    start, arrive, finish = band_copies(lambda band: surface, surfaces, band_sems)
    start()

    def rest(k, carry):
        level(k)
        return carry

    lax.fori_loop(1, levels, rest, 0)
    for copy in lon_copies(0, lons):
        copy.wait_send()

    def drain(k, carry):
        lat_sent(k, lats)
        return carry

    lax.fori_loop(0, levels + 1, drain, 0)
    arrive()
    source_ref[...] = surfaces[...]
    finish()


def adjoint_kernel(
    adjoint_ref,
    sums_ref,
    fixed_ref,
    increment_ref,
    gradient_ref,
    field,
    returns,
    lon_sent,
    lon_came,
    lat_sent_ref,
    lat_came_ref,
    lon_sems,
    lat_sems,
    band_sems,
):
    levels, height, width = increment_ref.shape
    pairs = levels // 2
    greet(*edges())
    start, arrive, finish = band_copies(lambda band: sums_ref.at[band], returns, band_sems)
    start()
    lons = (lon_sent, lon_came, lon_sems)
    lats = (lat_sent_ref, lat_came_ref, lat_sems)
    rows = pl.ds(0, height)
    own = rows, pl.ds(0, width)
    side = rows, pl.ds(width, LANES)
    ends = pl.ds(height, 2 * HALO)
    lon_pack(lon_sent, 0, [adjoint_ref[k] for k in range(1, levels)])
    for copy in lon_copies(0, lons):
        copy.start()

    def fill(k, carry):
        field[(k,) + own] = adjoint_ref[k]
        return carry

    lax.fori_loop(1, levels, fill, 0)
    for copy in lon_copies(0, lons):
        copy.wait_recv()
    for k in range(1, levels):
        field[(k,) + side] = lon_unpack(lon_came, 0, k - 1)

    def send(pair, carry):
        first = field[2 * pair - 1, rows, :]
        second = field[jnp.minimum(2 * pair, levels - 1), rows, :]
        lat_pack(lat_sent_ref, pair, first, second)
        lat_start(pair, lats)
        return carry

    lax.fori_loop(1, pairs + 1, send, 0)
    arrive()

    def add(band, total):
        return total + returns[band]

    total = lax.fori_loop(1, returns.shape[0], add, returns[0])
    mask = fixed_ref[(levels,) + own]
    first = adjoint_ref[0] + mask * plane_of(total, height)
    lon_pack(lon_sent, 1, [first])
    for copy in lon_copies(1, lons):
        copy.start()
    field[(0,) + own] = first

    def sweep(k):
        coefficients = coefficients_of(fixed_ref[k], fixed_ref[levels])
        value = field[k]
        for _ in range(NSTEP):
            value = stepped(value, coefficients)
        gradient_ref[k] = value[:height, :width] + increment_ref[k]

    def couple_of(pair, carry):
        later = jnp.minimum(2 * pair, levels - 1)
        upper, lower = lat_came(pair, lats)
        field[later, ends, :] = lower
        field[2 * pair - 1, ends, :] = upper
        sweep(2 * pair - 1)
        pl.when(2 * pair < levels)(lambda: sweep(later))
        return carry

    lax.fori_loop(1, pairs // 2 + 1, couple_of, 0)
    for copy in lon_copies(1, lons):
        copy.wait_recv()
    field[(0,) + side] = lon_unpack(lon_came, 1, 0)
    wide = field[0, rows, :]
    lat_pack(lat_sent_ref, 0, wide, wide)
    lat_start(0, lats)
    lax.fori_loop(pairs // 2 + 1, pairs + 1, couple_of, 0)
    field[0, ends, :] = lat_came(0, lats)[0]
    sweep(0)
    for at in range(2):
        for copy in lon_copies(at, lons):
            copy.wait_send()

    def drain(k, carry):
        lat_sent(k, lats)
        return carry

    lax.fori_loop(0, pairs + 1, drain, 0)
    finish()


def local(
    increment, diffusivity, innovation, land_mask, pull_cells, put_cells, pull_weight, pull_count
):
    levels, height, width = increment.shape[1:]
    bands = lax.axis_size("lat")
    rows = height * width // LANES
    lines = pull_cells.shape[-1] // LANES
    tall, wide = height + 2 * HALO, width + LANES
    pairs = levels // 2
    whole = pl.BlockSpec(memory_space=pltpu.VMEM)
    space = 48 * 1024 * 1024

    def real(*shape):
        return jax.ShapeDtypeStruct(shape, jnp.float32)

    def room(*shape):
        return pltpu.VMEM(shape, jnp.float32)

    def halos(sides, messages):
        return [
            room(sides, 2, height, LANES),
            room(sides, 2, height, LANES),
            room(messages, 2, 2 * HALO, wide),
            room(messages, 2, 2 * HALO, wide),
            pltpu.SemaphoreType.DMA((2, sides, 2)),
            pltpu.SemaphoreType.DMA((2, messages, 2)),
            pltpu.SemaphoreType.DMA((2, bands)),
        ]

    block = real(levels, height, width)
    slots = jax.ShapeDtypeStruct((bands, lines, LANES), jnp.int32)
    state, fixed, source, pull, put, weight = pl.pallas_call(
        forward_kernel,
        out_shape=(block, real(levels + 1, tall, wide), real(bands, rows, LANES))
        + (slots, slots, real(bands, lines, LANES)),
        in_specs=[whole] * 6,
        out_specs=(whole,) * 6,
        scratch_shapes=[room(levels, tall, wide), room(rows, LANES), room(bands, rows, LANES)]
        + halos(1, levels + 1),
        compiler_params=pltpu.CompilerParams(
            vmem_limit_bytes=space, collective_id=0, has_side_effects=True
        ),
    )(
        increment[0],
        diffusivity[0],
        land_mask,
        pull_cells.reshape(bands, -1),
        put_cells.reshape(bands, -1),
        pull_weight.reshape(bands, -1),
    )

    linear, adjoint, sums = pl.pallas_call(
        functools.partial(couple_kernel, height, width),
        out_shape=(block, block, real(bands, rows, LANES)),
        in_specs=[pl.BlockSpec(memory_space=pltpu.SMEM)] + [whole] * 7,
        out_specs=(whole, whole, whole),
        scratch_shapes=[room(2 * rows, LANES), room(rows, LANES)],
        compiler_params=pltpu.CompilerParams(vmem_limit_bytes=space),
    )(
        pull_count,
        source,
        pull,
        put,
        weight,
        land_mask,
        state,
        innovation[0],
    )

    gradient = pl.pallas_call(
        adjoint_kernel,
        out_shape=block,
        in_specs=[whole] * 4,
        out_specs=whole,
        scratch_shapes=[room(levels, tall, wide), room(bands, rows, LANES)]
        + halos(2, pairs + 1),
        compiler_params=pltpu.CompilerParams(
            vmem_limit_bytes=space, collective_id=1, has_side_effects=True
        ),
    )(adjoint, sums, fixed, increment[0])
    return (linear[None], gradient[None])


def solution(mesh):
    placed = (
        P("comp", None, "lat", "lon"),
        P("comp", None, "lat", "lon"),
        P("comp", None, "lat", "lon"),
        P("lat", "lon"),
        P("comp", "lat", "lon", None, None),
        P("comp", "lat", "lon", None, None),
        P("comp", "lat", "lon", None, None),
        P("comp", "lat", "lon", None),
    )
    return jax.shard_map(
        local,
        mesh=mesh,
        in_specs=placed,
        out_specs=(P("comp", None, "lat", "lon"), P("comp", None, "lat", "lon")),
        check_vma=False,
    )
```

```python
import functools

import jax
import jax.numpy as jnp
from jax import lax
from jax.experimental import pallas as pl
from jax.experimental.pallas import tpu as pltpu
from jax.sharding import PartitionSpec as P

NSTEP = 4
LANES = 128
HALO = 4
MESH = pl.DeviceIdType.MESH


def shifted(value, amount, axis):
    return pltpu.roll(value, amount % value.shape[axis], axis)


def coefficients_of(diffusivity, mask):
    half = mask * 0.5
    pairs = ((-1, 1), (1, 1), (1, 0), (-1, 0))
    return [
        half * shifted(mask, by, axis) * (diffusivity + shifted(diffusivity, by, axis))
        for by, axis in pairs
    ]


def stepped(field, coefficients):
    east, west, south, north = coefficients
    change = east * (shifted(field, -1, 1) - field) + west * (shifted(field, 1, 1) - field)
    change = change + south * (shifted(field, 1, 0) - field)
    change = change + north * (shifted(field, -1, 0) - field)
    return field + change


def table_of(plane):
    parts = [plane[:, at : at + LANES] for at in range(0, plane.shape[1], LANES)]
    return jnp.concatenate(parts, axis=0)


def plane_of(table, height):
    parts = [table[at : at + height] for at in range(0, table.shape[0], height)]
    return jnp.concatenate(parts, axis=1)


def split_cell(cell, height, width):
    row = cell // width
    column = cell - row * width
    tile = column // LANES
    return tile * height + row, column - tile * LANES


def looked_up(table_ref, index, high, low):
    rows = table_ref.shape[-2]

    def one(row, found):
        line = jnp.broadcast_to(table_ref[index + (pl.ds(row, 1), slice(None))], low.shape)
        return jnp.where(high == row, jnp.take_along_axis(line, low, axis=1, mode="promise_in_bounds"), found)

    found = jnp.zeros(low.shape, jnp.float32)
    for row in range(rows):
        found = one(row, found)
    return found


def spread(values, high, low, rows):
    narrow = jnp.bfloat16
    pack = 16

    def lined(row, count):
        tile = jnp.broadcast_to(row.astype(jnp.float32), (pack, LANES)).astype(narrow)
        return jnp.concatenate([tile] * (count // pack), axis=0)

    first = values.astype(narrow).astype(jnp.float32)
    second = values - first
    row_at = lax.broadcasted_iota(jnp.int32, (rows, LANES), 0).astype(jnp.float32).astype(narrow)
    lane_at = lax.broadcasted_iota(jnp.int32, (LANES, LANES), 0).astype(jnp.float32).astype(narrow)
    one, zero = jnp.ones((), narrow), jnp.zeros((), narrow)
    left, right = [], []
    for r in range(values.shape[0]):
        hit = lined(high[r : r + 1], rows) == row_at
        top = jnp.where(hit, lined(first[r : r + 1], rows), zero)
        bottom = jnp.where(hit, lined(second[r : r + 1], rows), zero)
        left.append(jnp.concatenate([top, bottom], axis=0))
        right.append(jnp.where(lined(low[r : r + 1], LANES) == lane_at, one, zero))
    return lax.dot_general(
        jnp.concatenate(left, axis=1),
        jnp.concatenate(right, axis=1),
        (((1,), (1,)), ((), ())),
        preferred_element_type=jnp.float32,
    )


def couple_kernel(
    height,
    width,
    count_ref,
    source_ref,
    pull_ref,
    put_ref,
    weight_ref,
    land_ref,
    state_ref,
    innovation_ref,
    linear_ref,
    adjoint_ref,
    sums_ref,
    total_ref,
    residual_ref,
):
    bands = source_ref.shape[0]
    lines = pull_ref.shape[1]
    rows = height * width // LANES
    deep = min(16, lines)
    block = deep * LANES
    slot = lax.broadcasted_iota(jnp.int32, (deep, LANES), 0) * LANES
    slot = slot + lax.broadcasted_iota(jnp.int32, (deep, LANES), 1)

    def slots(band, at):
        where = pl.ds(pl.multiple_of(at * deep, deep), deep)
        pull = split_cell(pull_ref[band, where, :], height, width)
        put = split_cell(put_ref[band, where, :], height, width)
        live = slot + at * block < count_ref[0, 0, 0, band]
        return pull, put, jnp.where(live, weight_ref[band, where, :], 0.0)

    def blocks(band):
        return (count_ref[0, 0, 0, band] + block - 1) // block

    total_ref[...] = jnp.zeros_like(total_ref)

    def forward_band(band, carry):
        def body(at, carry):
            pull, put, weight = slots(band, at)
            values = weight * looked_up(source_ref, (band,), *pull)
            total_ref[...] += spread(values, *put, rows)
            return carry

        return lax.fori_loop(0, blocks(band), body, carry)

    lax.fori_loop(0, bands, forward_band, 0)
    ocean = lax.axis_index("comp") == 1
    mask = jnp.where(ocean, land_ref[...].astype(jnp.float32), 1.0)
    income = plane_of(total_ref[:rows] + total_ref[rows:], height)
    linear_ref[...] = state_ref[...]
    linear_ref[0] = state_ref[0] + mask * income
    adjoint_ref[...] = linear_ref[...] - innovation_ref[...]
    residual_ref[...] = table_of(mask * adjoint_ref[0])

    def backward_band(band, carry):
        total_ref[...] = jnp.zeros_like(total_ref)

        def body(at, carry):
            pull, put, weight = slots(band, at)
            values = weight * looked_up(residual_ref, (), *put)
            total_ref[...] += spread(values, *pull, rows)
            return carry

        lax.fori_loop(0, blocks(band), body, 0)
        sums_ref[band] = total_ref[:rows] + total_ref[rows:]
        return carry

    lax.fori_loop(0, bands, backward_band, 0)


def place():
    comp, lat, lon = (lax.axis_index(name) for name in ("comp", "lat", "lon"))
    lats, lons = lax.axis_size("lat"), lax.axis_size("lon")
    return comp, lat, lon, lats, lons


def greet(has_south, has_north, at_fold):
    comp, lat, lon, lats, lons = place()
    barrier = pltpu.get_barrier_semaphore()

    def hail(*where):
        pl.semaphore_signal(barrier, inc=1, device_id=where, device_id_type=MESH)

    hail(comp, lat, lax.rem(lon + 1, lons))
    hail(comp, lat, lax.rem(lon + lons - 1, lons))
    pl.when(has_south)(lambda: hail(comp, lat - 1, lon))
    pl.when(has_north)(lambda: hail(comp, lat + 1, lon))
    pl.when(at_fold)(lambda: hail(comp, lat, lons - 1 - lon))

    def across(band, carry):
        hail(1 - comp, band, lon)
        return carry

    lax.fori_loop(0, lats, across, 0)
    rows = has_south.astype(jnp.int32) + has_north.astype(jnp.int32) + at_fold.astype(jnp.int32)
    pl.semaphore_wait(barrier, 2 + lats + rows)


def edges():
    comp, lat, lon, lats, lons = place()
    return lat > 0, lat < lats - 1, (comp == 1) & (lat == lats - 1)


def remote(source, target, sems, where):
    return pltpu.make_async_remote_copy(
        src_ref=source,
        dst_ref=target,
        send_sem=sems[0],
        recv_sem=sems[1],
        device_id=where,
        device_id_type=MESH,
    )


def lon_copies(at, buffers):
    sent, came, sems = buffers
    comp, lat, lon, lats, lons = place()
    ends = (lax.rem(lon + 1, lons), lax.rem(lon + lons - 1, lons))
    return [
        remote(
            sent.at[at, way],
            came.at[at, way],
            (sems.at[0, at, way], sems.at[1, at, way]),
            (comp, lat, ends[way]),
        )
        for way in range(2)
    ]


def lon_pack(sent, at, planes):
    lane = lax.broadcasted_iota(jnp.int32, (planes[0].shape[0], LANES), 1)
    ahead = jnp.zeros(lane.shape, jnp.float32)
    behind = jnp.zeros(lane.shape, jnp.float32)
    for k, plane in enumerate(planes):
        inside = (lane >= HALO * k) & (lane < HALO * (k + 1))
        tail = shifted(plane[:, plane.shape[1] - LANES :], HALO * k + HALO, 1)
        head = shifted(plane[:, :LANES], HALO * k, 1)
        ahead = jnp.where(inside, tail, ahead)
        behind = jnp.where(inside, head, behind)
    sent[at, 0] = ahead
    sent[at, 1] = behind


def lon_unpack(came, at, k):
    west, east = came[at, 0], came[at, 1]
    lane = lax.broadcasted_iota(jnp.int32, west.shape, 1)
    ends = jnp.where(lane >= LANES - HALO, shifted(west, -HALO * (k + 1), 1), 0.0)
    return jnp.where(lane < HALO, shifted(east, -HALO * k, 1), ends)


def mirrored(rows):
    tiles = []
    for at in range(0, rows.shape[1], LANES):
        tile = rows[:, at : at + LANES]
        for axis, bits in ((1, (1, 2, 4, 8, 16, 32, 64)), (0, (1, 2))):
            index = lax.broadcasted_iota(jnp.int32, tile.shape, axis)
            for bit in bits:
                odd = lax.rem(index // bit, 2) == 1
                tile = jnp.where(odd, shifted(tile, bit, axis), shifted(tile, -bit, axis))
        tiles.append(tile)
    own = tiles[-2::-1]
    return jnp.concatenate(own + tiles[-1:], axis=1)


def lat_copies(at, buffers):
    sent, came, sems = buffers
    comp, lat, lon, lats, lons = place()
    has_south, has_north, at_fold = edges()

    def one(way, slot, where):
        return remote(
            sent.at[at, way],
            came.at[at, slot],
            (sems.at[0, at, way], sems.at[1, at, slot]),
            where,
        )

    return (
        (has_north, one(0, 0, (comp, lat + 1, lon))),
        (has_south, one(1, 1, (comp, lat - 1, lon))),
        (at_fold, one(0, 1, (comp, lat, lons - 1 - lon))),
    )


def lat_start(at, buffers):
    for there, copy in lat_copies(at, buffers):
        pl.when(there)(copy.start)


def lat_sent(at, buffers):
    for there, copy in lat_copies(at, buffers):
        pl.when(there)(copy.wait_send)


def lat_came(at, buffers):
    came = buffers[1]
    has_south, has_north, at_fold = edges()
    up, down, fold = (copy for there, copy in lat_copies(at, buffers))
    pl.when(has_south)(up.wait_recv)
    pl.when(has_north)(down.wait_recv)
    pl.when(at_fold)(fold.wait_recv)

    @pl.when(at_fold)
    def _():
        came[at, 1] = mirrored(came[at, 1])

    @pl.when(jnp.logical_not(has_south))
    def _():
        came[at, 0] = jnp.zeros(came.shape[2:], jnp.float32)

    @pl.when(jnp.logical_not(has_north | at_fold))
    def _():
        came[at, 1] = jnp.zeros(came.shape[2:], jnp.float32)

    south, north = came[at, 0], came[at, 1]
    upper = jnp.concatenate([north[:HALO], south[:HALO]], axis=0)
    lower = jnp.concatenate([north[HALO:], south[HALO:]], axis=0)
    return upper, lower


def lat_pack(sent, at, first, second):
    top = first.shape[0] - HALO
    sent[at, 0] = jnp.concatenate([first[top:], second[top:]], axis=0)
    sent[at, 1] = jnp.concatenate([first[:HALO], second[:HALO]], axis=0)


def band_copies(source, came, sems):
    comp, lat, lon, lats, lons = place()

    def one(band):
        return remote(
            source(band), came.at[lat], (sems.at[0, band], sems.at[1, lat]), (1 - comp, band, lon)
        )

    def arrival(band):
        return remote(
            source(band), came.at[band], (sems.at[0, band], sems.at[1, band]), (1 - comp, band, lon)
        )

    def each(act):
        def body(band, carry):
            act(band)
            return carry

        lax.fori_loop(0, lats, body, 0)

    return (
        lambda: each(lambda band: one(band).start()),
        lambda: each(lambda band: arrival(band).wait_recv()),
        lambda: each(lambda band: one(band).wait_send()),
    )


def forward_kernel(
    increment_far,
    diffusivity_far,
    land_far,
    pull_far,
    put_far,
    weight_far,
    state_ref,
    fixed_ref,
    source_ref,
    pull_lines,
    put_lines,
    weight_lines,
    increment_ref,
    diffusivity_ref,
    land_ref,
    pull_ref,
    put_ref,
    weight_ref,
    load_sems,
    field,
    surface,
    surfaces,
    lon_sent,
    lon_came,
    lat_sent_ref,
    lat_came_ref,
    lon_sems,
    lat_sems,
    band_sems,
):
    levels, height, width = increment_ref.shape
    loads = [
        pltpu.make_async_copy(far, near, load_sems.at[at])
        for at, (far, near) in enumerate(
            (
                (increment_far, increment_ref),
                (diffusivity_far, diffusivity_ref),
                (land_far, land_ref),
                (pull_far, pull_ref),
                (put_far, put_ref),
                (weight_far, weight_ref),
            )
        )
    ]
    for load in loads:
        load.start()
    greet(*edges())
    for load in loads[:3]:
        load.wait()
    ocean = lax.axis_index("comp") == 1
    mask = jnp.where(ocean, land_ref[...].astype(jnp.float32), 1.0)
    lons = (lon_sent, lon_came, lon_sems)
    lats = (lat_sent_ref, lat_came_ref, lat_sems)
    planes = [increment_ref[k] for k in range(levels)]
    planes = planes + [diffusivity_ref[k] for k in range(levels)] + [mask]
    lon_pack(lon_sent, 0, planes)
    for copy in lon_copies(0, lons):
        copy.start()
    own = pl.ds(0, height), pl.ds(0, width)
    side = pl.ds(0, height), pl.ds(width, LANES)
    fixed_ref[(levels,) + own] = mask

    def fill(k, carry):
        field[(k,) + own] = increment_ref[k]
        fixed_ref[(k,) + own] = diffusivity_ref[k]
        return carry

    lax.fori_loop(0, levels, fill, 0)
    for load in loads[3:]:
        load.wait()
    for line in range(pull_lines.shape[1]):
        lanes = pl.ds(line * LANES, LANES)
        pull_lines[:, line, :] = pull_ref[:, lanes]
        put_lines[:, line, :] = put_ref[:, lanes]
        weight_lines[:, line, :] = weight_ref[:, lanes]
    for copy in lon_copies(0, lons):
        copy.wait_recv()
    for k in range(levels):
        field[(k,) + side] = lon_unpack(lon_came, 0, k)
        fixed_ref[(k,) + side] = lon_unpack(lon_came, 0, levels + k)
    fixed_ref[(levels,) + side] = lon_unpack(lon_came, 0, 2 * levels)

    wide_mask = fixed_ref[levels, pl.ds(0, height), :]
    lat_pack(lat_sent_ref, levels, wide_mask, wide_mask)
    lat_start(levels, lats)

    def send(k, carry):
        rows = pl.ds(0, height)
        lat_pack(lat_sent_ref, k, field[k, rows, :], fixed_ref[k, rows, :])
        lat_start(k, lats)
        return carry

    lax.fori_loop(0, levels, send, 0)
    ends = pl.ds(height, 2 * HALO)
    fixed_ref[levels, ends, :] = lat_came(levels, lats)[0]

    def level(k):
        field[k, ends, :], fixed_ref[k, ends, :] = lat_came(k, lats)
        coefficients = coefficients_of(fixed_ref[k], fixed_ref[levels])
        value = field[k]
        for _ in range(NSTEP):
            value = stepped(value, coefficients)
        state_ref[k] = value[:height, :width]

    level(0)
    surface[...] = table_of(mask * state_ref[0])
    start, arrive, finish = band_copies(lambda band: surface, surfaces, band_sems)
    start()

    def rest(k, carry):
        level(k)
        return carry

    lax.fori_loop(1, levels, rest, 0)
    for copy in lon_copies(0, lons):
        copy.wait_send()

    def drain(k, carry):
        lat_sent(k, lats)
        return carry

    lax.fori_loop(0, levels + 1, drain, 0)
    arrive()
    source_ref[...] = surfaces[...]
    finish()


def adjoint_kernel(
    adjoint_ref,
    sums_ref,
    fixed_ref,
    increment_ref,
    gradient_ref,
    field,
    returns,
    lon_sent,
    lon_came,
    lat_sent_ref,
    lat_came_ref,
    lon_sems,
    lat_sems,
    band_sems,
):
    levels, height, width = increment_ref.shape
    pairs = levels // 2
    greet(*edges())
    start, arrive, finish = band_copies(lambda band: sums_ref.at[band], returns, band_sems)
    start()
    lons = (lon_sent, lon_came, lon_sems)
    lats = (lat_sent_ref, lat_came_ref, lat_sems)
    rows = pl.ds(0, height)
    own = rows, pl.ds(0, width)
    side = rows, pl.ds(width, LANES)
    ends = pl.ds(height, 2 * HALO)
    lon_pack(lon_sent, 0, [adjoint_ref[k] for k in range(1, levels)])
    for copy in lon_copies(0, lons):
        copy.start()

    def fill(k, carry):
        field[(k,) + own] = adjoint_ref[k]
        return carry

    lax.fori_loop(1, levels, fill, 0)
    for copy in lon_copies(0, lons):
        copy.wait_recv()
    for k in range(1, levels):
        field[(k,) + side] = lon_unpack(lon_came, 0, k - 1)

    def send(pair, carry):
        first = field[2 * pair - 1, rows, :]
        second = field[jnp.minimum(2 * pair, levels - 1), rows, :]
        lat_pack(lat_sent_ref, pair, first, second)
        lat_start(pair, lats)
        return carry

    lax.fori_loop(1, pairs + 1, send, 0)
    arrive()

    def add(band, total):
        return total + returns[band]

    total = lax.fori_loop(1, returns.shape[0], add, returns[0])
    mask = fixed_ref[(levels,) + own]
    first = adjoint_ref[0] + mask * plane_of(total, height)
    lon_pack(lon_sent, 1, [first])
    for copy in lon_copies(1, lons):
        copy.start()
    field[(0,) + own] = first

    def sweep(k):
        coefficients = coefficients_of(fixed_ref[k], fixed_ref[levels])
        value = field[k]
        for _ in range(NSTEP):
            value = stepped(value, coefficients)
        gradient_ref[k] = value[:height, :width] + increment_ref[k]

    def couple_of(pair, carry):
        later = jnp.minimum(2 * pair, levels - 1)
        upper, lower = lat_came(pair, lats)
        field[later, ends, :] = lower
        field[2 * pair - 1, ends, :] = upper
        sweep(2 * pair - 1)
        pl.when(2 * pair < levels)(lambda: sweep(later))
        return carry

    lax.fori_loop(1, pairs // 2 + 1, couple_of, 0)
    for copy in lon_copies(1, lons):
        copy.wait_recv()
    field[(0,) + side] = lon_unpack(lon_came, 1, 0)
    wide = field[0, rows, :]
    lat_pack(lat_sent_ref, 0, wide, wide)
    lat_start(0, lats)
    lax.fori_loop(pairs // 2 + 1, pairs + 1, couple_of, 0)
    field[0, ends, :] = lat_came(0, lats)[0]
    sweep(0)
    for at in range(2):
        for copy in lon_copies(at, lons):
            copy.wait_send()

    def drain(k, carry):
        lat_sent(k, lats)
        return carry

    lax.fori_loop(0, pairs + 1, drain, 0)
    finish()


def local(
    increment, diffusivity, innovation, land_mask, pull_cells, put_cells, pull_weight, pull_count
):
    levels, height, width = increment.shape[1:]
    bands = lax.axis_size("lat")
    rows = height * width // LANES
    lines = pull_cells.shape[-1] // LANES
    tall, wide = height + 2 * HALO, width + LANES
    pairs = levels // 2
    whole = pl.BlockSpec(memory_space=pltpu.VMEM)
    space = 62 * 1024 * 1024

    def real(*shape):
        return jax.ShapeDtypeStruct(shape, jnp.float32)

    def room(*shape):
        return pltpu.VMEM(shape, jnp.float32)

    def halos(sides, messages):
        return [
            room(sides, 2, height, LANES),
            room(sides, 2, height, LANES),
            room(messages, 2, 2 * HALO, wide),
            room(messages, 2, 2 * HALO, wide),
            pltpu.SemaphoreType.DMA((2, sides, 2)),
            pltpu.SemaphoreType.DMA((2, messages, 2)),
            pltpu.SemaphoreType.DMA((2, bands)),
        ]

    block = real(levels, height, width)
    slots = jax.ShapeDtypeStruct((bands, lines, LANES), jnp.int32)
    state, fixed, source, pull, put, weight = pl.pallas_call(
        forward_kernel,
        out_shape=(block, real(levels + 1, tall, wide), real(bands, rows, LANES))
        + (slots, slots, real(bands, lines, LANES)),
        in_specs=[pl.BlockSpec(memory_space=pltpu.HBM)] * 6,
        out_specs=(whole,) * 6,
        scratch_shapes=[
            room(levels, height, width),
            room(levels, height, width),
            pltpu.VMEM((height, width), jnp.int32),
            pltpu.VMEM((bands, lines * LANES), jnp.int32),
            pltpu.VMEM((bands, lines * LANES), jnp.int32),
            room(bands, lines * LANES),
            pltpu.SemaphoreType.DMA((6,)),
        ]
        + [room(levels, tall, wide), room(rows, LANES), room(bands, rows, LANES)]
        + halos(1, levels + 1),
        compiler_params=pltpu.CompilerParams(
            vmem_limit_bytes=space, collective_id=0, has_side_effects=True
        ),
    )(
        increment[0],
        diffusivity[0],
        land_mask,
        pull_cells.reshape(bands, -1),
        put_cells.reshape(bands, -1),
        pull_weight.reshape(bands, -1),
    )

    linear, adjoint, sums = pl.pallas_call(
        functools.partial(couple_kernel, height, width),
        out_shape=(block, block, real(bands, rows, LANES)),
        in_specs=[pl.BlockSpec(memory_space=pltpu.SMEM)] + [whole] * 7,
        out_specs=(whole, whole, whole),
        scratch_shapes=[room(2 * rows, LANES), room(rows, LANES)],
        compiler_params=pltpu.CompilerParams(vmem_limit_bytes=space),
    )(
        pull_count,
        source,
        pull,
        put,
        weight,
        land_mask,
        state,
        innovation[0],
    )

    gradient = pl.pallas_call(
        adjoint_kernel,
        out_shape=block,
        in_specs=[whole] * 4,
        out_specs=whole,
        scratch_shapes=[room(levels, tall, wide), room(bands, rows, LANES)]
        + halos(2, pairs + 1),
        compiler_params=pltpu.CompilerParams(
            vmem_limit_bytes=space, collective_id=1, has_side_effects=True
        ),
    )(adjoint, sums, fixed, increment[0])
    return (linear[None], gradient[None])


def solution(mesh):
    placed = (
        P("comp", None, "lat", "lon"),
        P("comp", None, "lat", "lon"),
        P("comp", None, "lat", "lon"),
        P("lat", "lon"),
        P("comp", "lat", "lon", None, None),
        P("comp", "lat", "lon", None, None),
        P("comp", "lat", "lon", None, None),
        P("comp", "lat", "lon", None),
    )
    return jax.shard_map(
        local,
        mesh=mesh,
        in_specs=placed,
        out_specs=(P("comp", None, "lat", "lon"), P("comp", None, "lat", "lon")),
        check_vma=False,
    )
```

```python
import functools

import jax
import jax.numpy as jnp
from jax import lax
from jax.experimental import pallas as pl
from jax.experimental.pallas import tpu as pltpu
from jax.sharding import PartitionSpec as P

NSTEP = 4
LANES = 128
HALO = 4
MESH = pl.DeviceIdType.MESH


def shifted(value, amount, axis):
    return pltpu.roll(value, amount % value.shape[axis], axis)


def coefficients_of(diffusivity, mask):
    half = mask * 0.5
    pairs = ((-1, 1), (1, 1), (1, 0), (-1, 0))
    return [
        half * shifted(mask, by, axis) * (diffusivity + shifted(diffusivity, by, axis))
        for by, axis in pairs
    ]


def stepped(field, coefficients):
    east, west, south, north = coefficients
    change = east * (shifted(field, -1, 1) - field) + west * (shifted(field, 1, 1) - field)
    change = change + south * (shifted(field, 1, 0) - field)
    change = change + north * (shifted(field, -1, 0) - field)
    return field + change


def table_of(plane):
    parts = [plane[:, at : at + LANES] for at in range(0, plane.shape[1], LANES)]
    return jnp.concatenate(parts, axis=0)


def plane_of(table, height):
    parts = [table[at : at + height] for at in range(0, table.shape[0], height)]
    return jnp.concatenate(parts, axis=1)


def split_cell(cell, height, width):
    row = cell // width
    column = cell - row * width
    tile = column // LANES
    return tile * height + row, column - tile * LANES


def looked_up(table_ref, index, high, low):
    rows = table_ref.shape[-2]

    def one(row, found):
        line = jnp.broadcast_to(table_ref[index + (pl.ds(row, 1), slice(None))], low.shape)
        return jnp.where(high == row, jnp.take_along_axis(line, low, axis=1, mode="promise_in_bounds"), found)

    found = jnp.zeros(low.shape, jnp.float32)
    for row in range(rows):
        found = one(row, found)
    return found


def spread(values, high, low, rows):
    narrow = jnp.bfloat16
    pack = 16

    def lined(row, count):
        tile = jnp.broadcast_to(row.astype(jnp.float32), (pack, LANES)).astype(narrow)
        return jnp.concatenate([tile] * (count // pack), axis=0)

    first = values.astype(narrow).astype(jnp.float32)
    second = values - first
    row_at = lax.broadcasted_iota(jnp.int32, (rows, LANES), 0).astype(jnp.float32).astype(narrow)
    lane_at = lax.broadcasted_iota(jnp.int32, (LANES, LANES), 0).astype(jnp.float32).astype(narrow)
    one, zero = jnp.ones((), narrow), jnp.zeros((), narrow)
    left, right = [], []
    for r in range(values.shape[0]):
        hit = lined(high[r : r + 1], rows) == row_at
        top = jnp.where(hit, lined(first[r : r + 1], rows), zero)
        bottom = jnp.where(hit, lined(second[r : r + 1], rows), zero)
        left.append(jnp.concatenate([top, bottom], axis=0))
        right.append(jnp.where(lined(low[r : r + 1], LANES) == lane_at, one, zero))
    return lax.dot_general(
        jnp.concatenate(left, axis=1),
        jnp.concatenate(right, axis=1),
        (((1,), (1,)), ((), ())),
        preferred_element_type=jnp.float32,
    )


def couple_kernel(
    height,
    width,
    count_ref,
    source_ref,
    pull_ref,
    put_ref,
    weight_ref,
    land_ref,
    state_ref,
    innovation_ref,
    linear_ref,
    adjoint_ref,
    sums_ref,
    total_ref,
    residual_ref,
):
    bands = source_ref.shape[0]
    lines = pull_ref.shape[1]
    rows = height * width // LANES
    deep = min(16, lines)
    block = deep * LANES
    slot = lax.broadcasted_iota(jnp.int32, (deep, LANES), 0) * LANES
    slot = slot + lax.broadcasted_iota(jnp.int32, (deep, LANES), 1)

    def slots(band, at):
        where = pl.ds(pl.multiple_of(at * deep, deep), deep)
        pull = split_cell(pull_ref[band, where, :], height, width)
        put = split_cell(put_ref[band, where, :], height, width)
        live = slot + at * block < count_ref[band]
        return pull, put, jnp.where(live, weight_ref[band, where, :], 0.0)

    def blocks(band):
        return (count_ref[band] + block - 1) // block

    total_ref[...] = jnp.zeros_like(total_ref)

    def forward_band(band, carry):
        def body(at, carry):
            pull, put, weight = slots(band, at)
            values = weight * looked_up(source_ref, (band,), *pull)
            total_ref[...] += spread(values, *put, rows)
            return carry

        return lax.fori_loop(0, blocks(band), body, carry)

    lax.fori_loop(0, bands, forward_band, 0)
    ocean = lax.axis_index("comp") == 1
    mask = jnp.where(ocean, land_ref[...].astype(jnp.float32), 1.0)
    income = plane_of(total_ref[:rows] + total_ref[rows:], height)
    linear_ref[...] = state_ref[...]
    linear_ref[0] = state_ref[0] + mask * income
    adjoint_ref[...] = linear_ref[...] - innovation_ref[...]
    residual_ref[...] = table_of(mask * adjoint_ref[0])

    def backward_band(band, carry):
        total_ref[...] = jnp.zeros_like(total_ref)

        def body(at, carry):
            pull, put, weight = slots(band, at)
            values = weight * looked_up(residual_ref, (), *put)
            total_ref[...] += spread(values, *pull, rows)
            return carry

        lax.fori_loop(0, blocks(band), body, 0)
        sums_ref[band] = total_ref[:rows] + total_ref[rows:]
        return carry

    lax.fori_loop(0, bands, backward_band, 0)


def place():
    comp, lat, lon = (lax.axis_index(name) for name in ("comp", "lat", "lon"))
    lats, lons = lax.axis_size("lat"), lax.axis_size("lon")
    return comp, lat, lon, lats, lons


def greet(has_south, has_north, at_fold):
    comp, lat, lon, lats, lons = place()
    barrier = pltpu.get_barrier_semaphore()

    def hail(*where):
        pl.semaphore_signal(barrier, inc=1, device_id=where, device_id_type=MESH)

    hail(comp, lat, lax.rem(lon + 1, lons))
    hail(comp, lat, lax.rem(lon + lons - 1, lons))
    pl.when(has_south)(lambda: hail(comp, lat - 1, lon))
    pl.when(has_north)(lambda: hail(comp, lat + 1, lon))
    pl.when(at_fold)(lambda: hail(comp, lat, lons - 1 - lon))

    def across(band, carry):
        hail(1 - comp, band, lon)
        return carry

    lax.fori_loop(0, lats, across, 0)
    rows = has_south.astype(jnp.int32) + has_north.astype(jnp.int32) + at_fold.astype(jnp.int32)
    pl.semaphore_wait(barrier, 2 + lats + rows)


def edges():
    comp, lat, lon, lats, lons = place()
    return lat > 0, lat < lats - 1, (comp == 1) & (lat == lats - 1)


def remote(source, target, sems, where):
    return pltpu.make_async_remote_copy(
        src_ref=source,
        dst_ref=target,
        send_sem=sems[0],
        recv_sem=sems[1],
        device_id=where,
        device_id_type=MESH,
    )


def lon_copies(at, buffers):
    sent, came, sems = buffers
    comp, lat, lon, lats, lons = place()
    ends = (lax.rem(lon + 1, lons), lax.rem(lon + lons - 1, lons))
    return [
        remote(
            sent.at[at, way],
            came.at[at, way],
            (sems.at[0, at, way], sems.at[1, at, way]),
            (comp, lat, ends[way]),
        )
        for way in range(2)
    ]


def lon_pack(sent, at, planes):
    lane = lax.broadcasted_iota(jnp.int32, (planes[0].shape[0], LANES), 1)
    ahead = jnp.zeros(lane.shape, jnp.float32)
    behind = jnp.zeros(lane.shape, jnp.float32)
    for k, plane in enumerate(planes):
        inside = (lane >= HALO * k) & (lane < HALO * (k + 1))
        tail = shifted(plane[:, plane.shape[1] - LANES :], HALO * k + HALO, 1)
        head = shifted(plane[:, :LANES], HALO * k, 1)
        ahead = jnp.where(inside, tail, ahead)
        behind = jnp.where(inside, head, behind)
    sent[at, 0] = ahead
    sent[at, 1] = behind


def lon_unpack(came, at, k):
    west, east = came[at, 0], came[at, 1]
    lane = lax.broadcasted_iota(jnp.int32, west.shape, 1)
    ends = jnp.where(lane >= LANES - HALO, shifted(west, -HALO * (k + 1), 1), 0.0)
    return jnp.where(lane < HALO, shifted(east, -HALO * k, 1), ends)


def mirrored(rows):
    tiles = []
    for at in range(0, rows.shape[1], LANES):
        tile = rows[:, at : at + LANES]
        for axis, bits in ((1, (1, 2, 4, 8, 16, 32, 64)), (0, (1, 2))):
            index = lax.broadcasted_iota(jnp.int32, tile.shape, axis)
            for bit in bits:
                odd = lax.rem(index // bit, 2) == 1
                tile = jnp.where(odd, shifted(tile, bit, axis), shifted(tile, -bit, axis))
        tiles.append(tile)
    own = tiles[-2::-1]
    return jnp.concatenate(own + tiles[-1:], axis=1)


def lat_copies(at, buffers):
    sent, came, sems = buffers
    comp, lat, lon, lats, lons = place()
    has_south, has_north, at_fold = edges()

    def one(way, slot, where):
        return remote(
            sent.at[at, way],
            came.at[at, slot],
            (sems.at[0, at, way], sems.at[1, at, slot]),
            where,
        )

    return (
        (has_north, one(0, 0, (comp, lat + 1, lon))),
        (has_south, one(1, 1, (comp, lat - 1, lon))),
        (at_fold, one(0, 1, (comp, lat, lons - 1 - lon))),
    )


def lat_start(at, buffers):
    for there, copy in lat_copies(at, buffers):
        pl.when(there)(copy.start)


def lat_sent(at, buffers):
    for there, copy in lat_copies(at, buffers):
        pl.when(there)(copy.wait_send)


def lat_came(at, buffers):
    came = buffers[1]
    has_south, has_north, at_fold = edges()
    up, down, fold = (copy for there, copy in lat_copies(at, buffers))
    pl.when(has_south)(up.wait_recv)
    pl.when(has_north)(down.wait_recv)
    pl.when(at_fold)(fold.wait_recv)

    @pl.when(at_fold)
    def _():
        came[at, 1] = mirrored(came[at, 1])

    @pl.when(jnp.logical_not(has_south))
    def _():
        came[at, 0] = jnp.zeros(came.shape[2:], jnp.float32)

    @pl.when(jnp.logical_not(has_north | at_fold))
    def _():
        came[at, 1] = jnp.zeros(came.shape[2:], jnp.float32)

    south, north = came[at, 0], came[at, 1]
    upper = jnp.concatenate([north[:HALO], south[:HALO]], axis=0)
    lower = jnp.concatenate([north[HALO:], south[HALO:]], axis=0)
    return upper, lower


def lat_pack(sent, at, first, second):
    top = first.shape[0] - HALO
    sent[at, 0] = jnp.concatenate([first[top:], second[top:]], axis=0)
    sent[at, 1] = jnp.concatenate([first[:HALO], second[:HALO]], axis=0)


def band_copies(source, came, sems):
    comp, lat, lon, lats, lons = place()

    def one(band):
        return remote(
            source(band), came.at[lat], (sems.at[0, band], sems.at[1, lat]), (1 - comp, band, lon)
        )

    def arrival(band):
        return remote(
            source(band), came.at[band], (sems.at[0, band], sems.at[1, band]), (1 - comp, band, lon)
        )

    def each(act):
        def body(band, carry):
            act(band)
            return carry

        lax.fori_loop(0, lats, body, 0)

    return (
        lambda: each(lambda band: one(band).start()),
        lambda: each(lambda band: arrival(band).wait_recv()),
        lambda: each(lambda band: one(band).wait_send()),
    )


def forward_kernel(
    increment_ref,
    diffusivity_ref,
    land_ref,
    state_ref,
    fixed_ref,
    source_ref,
    field,
    surface,
    surfaces,
    lon_sent,
    lon_came,
    lat_sent_ref,
    lat_came_ref,
    lon_sems,
    lat_sems,
    band_sems,
):
    levels, height, width = increment_ref.shape
    greet(*edges())
    ocean = lax.axis_index("comp") == 1
    mask = jnp.where(ocean, land_ref[...].astype(jnp.float32), 1.0)
    lons = (lon_sent, lon_came, lon_sems)
    lats = (lat_sent_ref, lat_came_ref, lat_sems)
    planes = [increment_ref[k] for k in range(levels)]
    planes = planes + [diffusivity_ref[k] for k in range(levels)] + [mask]
    lon_pack(lon_sent, 0, planes)
    for copy in lon_copies(0, lons):
        copy.start()
    own = pl.ds(0, height), pl.ds(0, width)
    side = pl.ds(0, height), pl.ds(width, LANES)
    fixed_ref[(levels,) + own] = mask

    def fill(k, carry):
        field[(k,) + own] = increment_ref[k]
        fixed_ref[(k,) + own] = diffusivity_ref[k]
        return carry

    lax.fori_loop(0, levels, fill, 0)
    for copy in lon_copies(0, lons):
        copy.wait_recv()
    for k in range(levels):
        field[(k,) + side] = lon_unpack(lon_came, 0, k)
        fixed_ref[(k,) + side] = lon_unpack(lon_came, 0, levels + k)
    fixed_ref[(levels,) + side] = lon_unpack(lon_came, 0, 2 * levels)

    wide_mask = fixed_ref[levels, pl.ds(0, height), :]
    lat_pack(lat_sent_ref, levels, wide_mask, wide_mask)
    lat_start(levels, lats)

    def send(k, carry):
        rows = pl.ds(0, height)
        lat_pack(lat_sent_ref, k, field[k, rows, :], fixed_ref[k, rows, :])
        lat_start(k, lats)
        return carry

    lax.fori_loop(0, levels, send, 0)
    ends = pl.ds(height, 2 * HALO)
    fixed_ref[levels, ends, :] = lat_came(levels, lats)[0]

    def level(k):
        field[k, ends, :], fixed_ref[k, ends, :] = lat_came(k, lats)
        coefficients = coefficients_of(fixed_ref[k], fixed_ref[levels])
        value = field[k]
        for _ in range(NSTEP):
            value = stepped(value, coefficients)
        state_ref[k] = value[:height, :width]

    level(0)
    surface[...] = table_of(mask * state_ref[0])
    start, arrive, finish = band_copies(lambda band: surface, surfaces, band_sems)
    start()

    def rest(k, carry):
        level(k)
        return carry

    lax.fori_loop(1, levels, rest, 0)
    for copy in lon_copies(0, lons):
        copy.wait_send()

    def drain(k, carry):
        lat_sent(k, lats)
        return carry

    lax.fori_loop(0, levels + 1, drain, 0)
    arrive()
    source_ref[...] = surfaces[...]
    finish()


def adjoint_kernel(
    adjoint_ref,
    sums_ref,
    fixed_ref,
    increment_ref,
    gradient_ref,
    field,
    returns,
    lon_sent,
    lon_came,
    lat_sent_ref,
    lat_came_ref,
    lon_sems,
    lat_sems,
    band_sems,
):
    levels, height, width = increment_ref.shape
    pairs = levels // 2
    greet(*edges())
    start, arrive, finish = band_copies(lambda band: sums_ref.at[band], returns, band_sems)
    start()
    lons = (lon_sent, lon_came, lon_sems)
    lats = (lat_sent_ref, lat_came_ref, lat_sems)
    rows = pl.ds(0, height)
    own = rows, pl.ds(0, width)
    side = rows, pl.ds(width, LANES)
    ends = pl.ds(height, 2 * HALO)
    lon_pack(lon_sent, 0, [adjoint_ref[k] for k in range(1, levels)])
    for copy in lon_copies(0, lons):
        copy.start()

    def fill(k, carry):
        field[(k,) + own] = adjoint_ref[k]
        return carry

    lax.fori_loop(1, levels, fill, 0)
    for copy in lon_copies(0, lons):
        copy.wait_recv()
    for k in range(1, levels):
        field[(k,) + side] = lon_unpack(lon_came, 0, k - 1)

    def send(pair, carry):
        first = field[2 * pair - 1, rows, :]
        second = field[jnp.minimum(2 * pair, levels - 1), rows, :]
        lat_pack(lat_sent_ref, pair, first, second)
        lat_start(pair, lats)
        return carry

    lax.fori_loop(1, pairs + 1, send, 0)
    arrive()

    def add(band, total):
        return total + returns[band]

    total = lax.fori_loop(1, returns.shape[0], add, returns[0])
    mask = fixed_ref[(levels,) + own]
    first = adjoint_ref[0] + mask * plane_of(total, height)
    lon_pack(lon_sent, 1, [first])
    for copy in lon_copies(1, lons):
        copy.start()
    field[(0,) + own] = first

    def sweep(k):
        coefficients = coefficients_of(fixed_ref[k], fixed_ref[levels])
        value = field[k]
        for _ in range(NSTEP):
            value = stepped(value, coefficients)
        gradient_ref[k] = value[:height, :width] + increment_ref[k]

    def couple_of(pair, carry):
        later = jnp.minimum(2 * pair, levels - 1)
        upper, lower = lat_came(pair, lats)
        field[later, ends, :] = lower
        field[2 * pair - 1, ends, :] = upper
        sweep(2 * pair - 1)
        pl.when(2 * pair < levels)(lambda: sweep(later))
        return carry

    lax.fori_loop(1, pairs // 2 + 1, couple_of, 0)
    for copy in lon_copies(1, lons):
        copy.wait_recv()
    field[(0,) + side] = lon_unpack(lon_came, 1, 0)
    wide = field[0, rows, :]
    lat_pack(lat_sent_ref, 0, wide, wide)
    lat_start(0, lats)
    lax.fori_loop(pairs // 2 + 1, pairs + 1, couple_of, 0)
    field[0, ends, :] = lat_came(0, lats)[0]
    sweep(0)
    for at in range(2):
        for copy in lon_copies(at, lons):
            copy.wait_send()

    def drain(k, carry):
        lat_sent(k, lats)
        return carry

    lax.fori_loop(0, pairs + 1, drain, 0)
    finish()


def local(
    increment, diffusivity, innovation, land_mask, pull_cells, put_cells, pull_weight, pull_count
):
    levels, height, width = increment.shape[1:]
    bands = lax.axis_size("lat")
    rows = height * width // LANES
    lines = pull_cells.shape[-1] // LANES
    tall, wide = height + 2 * HALO, width + LANES
    pairs = levels // 2
    whole = pl.BlockSpec(memory_space=pltpu.VMEM)
    space = 48 * 1024 * 1024

    def real(*shape):
        return jax.ShapeDtypeStruct(shape, jnp.float32)

    def room(*shape):
        return pltpu.VMEM(shape, jnp.float32)

    def halos(sides, messages):
        return [
            room(sides, 2, height, LANES),
            room(sides, 2, height, LANES),
            room(messages, 2, 2 * HALO, wide),
            room(messages, 2, 2 * HALO, wide),
            pltpu.SemaphoreType.DMA((2, sides, 2)),
            pltpu.SemaphoreType.DMA((2, messages, 2)),
            pltpu.SemaphoreType.DMA((2, bands)),
        ]

    block = real(levels, height, width)
    state, fixed, source = pl.pallas_call(
        forward_kernel,
        out_shape=(block, real(levels + 1, tall, wide), real(bands, rows, LANES)),
        in_specs=[whole] * 3,
        out_specs=(whole,) * 3,
        scratch_shapes=[room(levels, tall, wide), room(rows, LANES), room(bands, rows, LANES)]
        + halos(1, levels + 1),
        compiler_params=pltpu.CompilerParams(
            vmem_limit_bytes=space, collective_id=0, has_side_effects=True
        ),
    )(increment[0], diffusivity[0], land_mask)

    linear, adjoint, sums = pl.pallas_call(
        functools.partial(couple_kernel, height, width),
        out_shape=(block, block, real(bands, rows, LANES)),
        in_specs=[pl.BlockSpec(memory_space=pltpu.SMEM)] + [whole] * 7,
        out_specs=(whole, whole, whole),
        scratch_shapes=[room(2 * rows, LANES), room(rows, LANES)],
        compiler_params=pltpu.CompilerParams(vmem_limit_bytes=space),
    )(
        pull_count.reshape(bands),
        source,
        pull_cells.reshape(bands, lines, LANES),
        put_cells.reshape(bands, lines, LANES),
        pull_weight.reshape(bands, lines, LANES),
        land_mask,
        state,
        innovation[0],
    )

    gradient = pl.pallas_call(
        adjoint_kernel,
        out_shape=block,
        in_specs=[whole] * 4,
        out_specs=whole,
        scratch_shapes=[room(levels, tall, wide), room(bands, rows, LANES)]
        + halos(2, pairs + 1),
        compiler_params=pltpu.CompilerParams(
            vmem_limit_bytes=space, collective_id=1, has_side_effects=True
        ),
    )(adjoint, sums, fixed, increment[0])
    return (linear[None], gradient[None])


def solution(mesh):
    placed = (
        P("comp", None, "lat", "lon"),
        P("comp", None, "lat", "lon"),
        P("comp", None, "lat", "lon"),
        P("lat", "lon"),
        P("comp", "lat", "lon", None, None),
        P("comp", "lat", "lon", None, None),
        P("comp", "lat", "lon", None, None),
        P("comp", "lat", "lon", None),
    )
    return jax.shard_map(
        local,
        mesh=mesh,
        in_specs=placed,
        out_specs=(P("comp", None, "lat", "lon"), P("comp", None, "lat", "lon")),
        check_vma=False,
    )
```
